512 devices in a mesh: lat: 128 (over z, y, core), ch: 4 (over x).
Axes of the slice: x: 4, y: 8, z: 8, core: 2. Of those that a mesh axis runs over, the one named last changes fastest.
Arguments:
- grid_field: bfloat16 [256, 512, 1440], P('ch', 'lat'), may hold values from -6 to 6
- order_slots: int32 [512], replicated, may hold values from 0 to 511, each once
- mix_weight: bfloat16 [256, 256], replicated, may hold values from -0.375 to 0.375
- degree_gain: float32 [256, 512], P('ch'), may hold values from 0.3 to 3
- cotangent: bfloat16 [256, 512, 1440], P('ch', 'lat'), may hold values from -6 to 6
Outputs:
- block_output: bfloat16 [256, 512, 1440], P('ch', 'lat')
- spectrum: bfloat16 [512, 2, 256, 512], P('lat', None, 'ch')
- grad_field: bfloat16 [256, 512, 1440], P('ch', 'lat')
- grad_mix: float32 [256, 256], P(None, 'ch')
- grad_gain: float32 [256, 512], P('ch')
The draws below stay inside these ranges and needn't reach their ends.
Inputs may be any that keep to these rules, and one draw needn't show every extreme that they name: `order_slots`: each order from 0 to 511 stands in exactly one slot.
All inputs are finite; a program needn't handle non-finite values.
Results may differ from the reference program's by a relative error of at most 0.02.
Values may be sent and summed in bfloat16 or wider, within the bound.
A program may use at most 128 MiB of HBM per device.

```python
import math
import jax
import jax.numpy as jnp
from jax import lax

C = 256
NLON = 1440
ORD_DEV = 4
MODES = 512
NLAT = 512
N_LAT = 128


def block_levels(rng, extent, cuts, smallest, largest):
    def one(position, parts):
        steps = jax.random.uniform(jax.random.fold_in(jax.random.fold_in(rng, 6), position), (parts,), jnp.float32, smallest / len(cuts), largest / len(cuts))
        return jnp.repeat(jnp.exp(steps), extent[position] // parts).reshape((-1,) + (1,) * (len(extent) - position - 1))

    gain = one(*cuts[0])
    for cut in cuts[1:]:
        gain = gain * one(*cut)
    return gain


def normal_values(rng, dims, width, most, cuts=(), held_as=jnp.bfloat16):
    array = jax.random.normal(rng, dims, jnp.float32) * width
    if len(cuts) > 0:
        array = block_levels(rng, dims, cuts, -0.22, 0.18) * array
    return jnp.clip(array, min=-most, max=most).astype(held_as)


def setup_inputs(seed: int = 0) -> dict:
    arg_keys = jax.random.split(jax.random.key(seed), 6)
    grid_field = normal_values(arg_keys[0], (C, NLAT, NLON), 1.0, 6.0, ((0, 4), (1, 128)))
    order_slots = jax.random.permutation(arg_keys[1], MODES).astype(jnp.int32)
    mix_weight = normal_values(arg_keys[2], (C, C), C ** -0.5, 0.375)
    degree_gain = jnp.clip(jnp.exp(math.log(3.0) - 2.3025851 * jax.random.uniform(arg_keys[3], (C, MODES), jnp.float32) ** block_levels(arg_keys[3], (C, MODES), ((0, 4),), -0.2, 0.2)), 0.3, 3.0)
    cotangent = normal_values(arg_keys[4], (C, NLAT, NLON), 1.0, 6.0, ((0, 4), (1, 128)))
    return dict(grid_field=grid_field, order_slots=order_slots, mix_weight=mix_weight, degree_gain=degree_gain, cotangent=cotangent)


renew_every = 32

def lat_angles(lat_count):
    rows = jnp.arange(lat_count, dtype=jnp.int32).astype(jnp.float32)
    theta = math.pi * (rows + 0.5) / lat_count
    return (jnp.cos(theta), jnp.sin(theta))

def long_table(order_slots, lon_count):
    points = jnp.arange(lon_count, dtype=jnp.int32)
    wrapped = points[:, None] * order_slots[None, :] % lon_count
    angle = wrapped.astype(jnp.float32) * (2.0 * math.pi / lon_count)
    factor = math.sqrt(2.0 / lon_count)
    table = jnp.stack([jnp.cos(angle) * factor, -jnp.sin(angle) * factor], axis=-1)
    halving = jnp.where(order_slots == 0, 0.5, 1.0).astype(jnp.float32)
    forward_tab = table.reshape(lon_count, -1).astype(jnp.bfloat16)
    inverse_tab = (table * halving[None, :, None]).reshape(lon_count, -1).astype(jnp.bfloat16)
    return (forward_tab, inverse_tab)

def legendre_rows(own_orders, lat_count, mode_count):
    cosines, lat_sines = lat_angles(lat_count)
    order_vals = own_orders.astype(jnp.float32)
    counter = jnp.arange(1, mode_count, dtype=jnp.int32).astype(jnp.float32)
    ratios = jnp.log((2.0 * counter - 1.0) / (2.0 * counter))
    partial_logs = jnp.concatenate([jnp.zeros((1,), jnp.float32), jnp.cumsum(ratios)])
    matches = jnp.arange(mode_count, dtype=jnp.int32)[None, :] == own_orders[:, None]
    picked = lax.optimization_barrier(jnp.sum(jnp.where(matches, partial_logs[None, :], 0.0), axis=1))
    log_start = 0.5 * (jnp.log(order_vals + 0.5) + picked)[:, None] + order_vals[:, None] * jnp.log(lat_sines)[None, :]
    order_col = order_vals[:, None]

    def advance(carry, unused):
        previous, current, scale, base = carry
        columns = []
        for offset in range(renew_every):
            factor = jnp.exp(0.5 * scale)
            columns.append(current * factor * factor)
            degree = order_col + (base + offset + 1).astype(jnp.float32)
            upper = jnp.sqrt((4.0 * degree * degree - 1.0) / (degree * degree - order_col * order_col))
            below = degree - 1.0
            lower = jnp.sqrt((below * below - order_col * order_col) / jnp.maximum(4.0 * below * below - 1.0, 1.0))
            following = upper * (cosines[None, :] * current - lower * previous)
            previous, current = (current, following)
        biggest = jnp.maximum(jnp.abs(previous), jnp.abs(current))
        shift = jnp.log(biggest)
        rescale = jnp.exp(-shift)
        return ((previous * rescale, current * rescale, scale + shift, base + renew_every), jnp.stack(columns, axis=-1))
    block_count = -(-mode_count // renew_every)
    start = (jnp.zeros_like(log_start), jnp.ones_like(log_start), log_start, jnp.zeros((), jnp.int32))
    final_carry, pieces = lax.scan(advance, start, None, length=block_count)
    values = jnp.transpose(pieces, (1, 2, 0, 3)).reshape(own_orders.shape[0], lat_count, -1)[:, :, :mode_count]
    live = jnp.arange(mode_count, dtype=jnp.int32)[None, :] < (mode_count - own_orders)[:, None]
    scaled = jnp.where(live[:, None, :], values, 0.0) * math.sqrt(math.pi / lat_count)
    return scaled.astype(jnp.bfloat16)

def gain_lookup(degree_gain, own_orders):
    padded = jnp.concatenate([degree_gain, jnp.zeros_like(degree_gain)], axis=1)

    def pick_rows(first):
        return lax.dynamic_slice_in_dim(padded, first, degree_gain.shape[1], 1)
    return jax.vmap(pick_rows)(own_orders)

def degree_sum(terms, own_orders):
    mode_count = terms.shape[2]
    padded = jnp.concatenate([jnp.zeros_like(terms), terms], axis=2)

    def place(row, order_value):
        return lax.dynamic_slice_in_dim(row, mode_count - order_value, mode_count, 1)
    return lax.optimization_barrier(jnp.sum(jax.vmap(place)(padded, own_orders), axis=0))

def gelu_value(values):
    return values * 0.5 * (1.0 + lax.erf(values * (1.0 / math.sqrt(2.0))))

def gelu_slope(values):
    normal_cdf = 0.5 * (1.0 + lax.erf(values * (1.0 / math.sqrt(2.0))))
    return normal_cdf + values * jnp.exp(-0.5 * values * values) * (1.0 / math.sqrt(2.0 * math.pi))

def reference(grid_field, order_slots, mix_weight, degree_gain, cotangent):
    forward_tab, inverse_tab = long_table(order_slots, NLON)
    cosines, lat_sines = lat_angles(NLAT)
    spectral = jnp.einsum('cjn,nq->cjq', grid_field.astype(jnp.float32), forward_tab.astype(jnp.float32))
    spectral = (spectral * lat_sines[None, :, None]).astype(jnp.bfloat16)
    slot_view = spectral.reshape(C, NLAT, MODES, 2)
    weight_full = mix_weight.astype(jnp.float32)

    def forward_block(block_index):
        own_orders = lax.dynamic_slice_in_dim(order_slots, block_index * ORD_DEV, ORD_DEV)
        legendre = legendre_rows(own_orders, NLAT, MODES).astype(jnp.float32)
        slot_part = lax.dynamic_slice_in_dim(slot_view, block_index * ORD_DEV, ORD_DEV, 2).astype(jnp.float32)
        coeffs = jnp.einsum('cjsr,sjk->srck', slot_part, legendre).astype(jnp.bfloat16)
        mixed_pre = jnp.einsum('srik,io->srok', coeffs.astype(jnp.float32), weight_full).astype(jnp.bfloat16)
        gain_rows = gain_lookup(degree_gain, own_orders)
        spectrum = (mixed_pre.astype(jnp.float32) * gain_rows[:, None]).astype(jnp.bfloat16)
        returned = jnp.einsum('srck,sjk->cjsr', spectrum.astype(jnp.float32), legendre).astype(jnp.bfloat16)
        return (coeffs, mixed_pre, spectrum, returned)
    block_ids = jnp.arange(N_LAT, dtype=jnp.int32)
    coeffs, mixed_pre, spectrum, returned = lax.map(forward_block, block_ids)
    returned = jnp.transpose(returned, (1, 2, 0, 3, 4)).reshape(C, NLAT, 2 * MODES)
    inner_sum = jnp.einsum('cjq,nq->cjn', returned.astype(jnp.float32), inverse_tab.astype(jnp.float32))
    block_output = (grid_field.astype(jnp.float32) + gelu_value(inner_sum)).astype(jnp.bfloat16)
    slope_grad = (cotangent.astype(jnp.float32) * gelu_slope(inner_sum)).astype(jnp.bfloat16)
    returned_grad = jnp.einsum('cjn,nq->cjq', slope_grad.astype(jnp.float32), inverse_tab.astype(jnp.float32))
    returned_grad = returned_grad.astype(jnp.bfloat16).reshape(C, NLAT, MODES, 2)

    def backward_block(inputs):
        block_index, coeff_block, pre_block = inputs
        own_orders = lax.dynamic_slice_in_dim(order_slots, block_index * ORD_DEV, ORD_DEV)
        legendre = legendre_rows(own_orders, NLAT, MODES).astype(jnp.float32)
        slot_part = lax.dynamic_slice_in_dim(returned_grad, block_index * ORD_DEV, ORD_DEV, 2).astype(jnp.float32)
        spec_grad = jnp.einsum('cjsr,sjk->srck', slot_part, legendre)
        gain_rows = gain_lookup(degree_gain, own_orders)
        pre_grad = (spec_grad * gain_rows[:, None]).astype(jnp.bfloat16)
        gain_part = degree_sum(lax.optimization_barrier(jnp.sum(spec_grad * pre_block.astype(jnp.float32), axis=1)), own_orders)
        mix_part = jnp.einsum('srik,srok->io', coeff_block.astype(jnp.float32), pre_grad.astype(jnp.float32))
        coeff_grad = jnp.einsum('srok,io->srik', pre_grad.astype(jnp.float32), weight_full).astype(jnp.bfloat16)
        spectral_grad = jnp.einsum('srck,sjk->cjsr', coeff_grad.astype(jnp.float32), legendre)
        spectral_grad = (spectral_grad * lat_sines[None, :, None, None]).astype(jnp.bfloat16)
        return (gain_part, mix_part, spectral_grad)
    gain_parts, mix_parts, spectral_grad = lax.map(backward_block, (block_ids, coeffs, mixed_pre))
    grad_gain = lax.optimization_barrier(jnp.sum(gain_parts, axis=0)) / math.sqrt(MODES)
    grad_mix = lax.optimization_barrier(jnp.sum(mix_parts, axis=0)) / MODES
    spectral_grad = jnp.transpose(spectral_grad, (1, 2, 0, 3, 4)).reshape(C, NLAT, 2 * MODES)
    field_term = jnp.einsum('cjq,nq->cjn', spectral_grad.astype(jnp.float32), forward_tab.astype(jnp.float32))
    grad_field = (cotangent.astype(jnp.float32) + field_term).astype(jnp.bfloat16)
    spectrum = spectrum.reshape(MODES, 2, C, MODES)
    return (block_output, spectrum, grad_field, grad_mix, grad_gain)
```

```python
import functools
import math

import jax
import jax.numpy as jnp
import numpy as np
from jax import lax
from jax.experimental import pallas as pl
from jax.experimental.pallas import tpu as pltpu
from jax.sharding import PartitionSpec as P

MESH = pl.DeviceIdType.MESH
BF, F32 = jnp.bfloat16, jnp.float32
CL, JL, NLON = 64, 4, 1440
NZ, NY, NC, NX = 8, 8, 2, 4
NLAT, MODES = 512, 512
RENEW = 32
VMEM_BYTES = 56 * 1024 * 1024
NN = (((1,), (0,)), ((), ()))
NT = (((1,), (1,)), ((), ()))
TN = (((0,), (0,)), ((), ()))


def dot(a, b, dims=NN):
    return lax.dot_general(a, b, dims, preferred_element_type=F32)


def half_angle(steps):
    turns = jnp.floor(steps * (1.0 / NLON) + 0.5)
    t = (steps - turns * NLON) * (math.pi / NLON)
    u = t * t
    s = t * (1.0 + u * (-1.0 / 6 + u * (1.0 / 120 + u * (-1.0 / 5040 + u * (1.0 / 362880 + u * (-1.0 / 39916800))))))
    c = 1.0 + u * (-0.5 + u * (1.0 / 24 + u * (-1.0 / 720 + u * (1.0 / 40320 + u * (-1.0 / 3628800 + u * (1.0 / 479001600))))))
    return 1.0 - 2.0 * s * s, 2.0 * s * c


def tables_kernel(slots_ref, logs_ref, mcol_ref, cosv_ref, logsin_ref, f_ref, l_ref, lt_ref, up_ref, low_ref, raw_ref):
    slot = lax.axis_index("lat") * NX + lax.axis_index("ch")
    order = slots_ref[slot]
    m = order.astype(F32)

    def long_rows(i, carry):
        rows = pl.ds(pl.multiple_of(i * 64, 64), 64)
        mc = jnp.broadcast_to(mcol_ref[rows, :].astype(F32), (64, 128))
        lane = lax.broadcasted_iota(jnp.int32, (64, 128), 1).astype(F32)
        cb, sb = half_angle(mc * lane)
        ca, sa = half_angle(mc * (lane * 128.0))
        cb, sb = cb * math.sqrt(2.0 / NLON), sb * math.sqrt(2.0 / NLON)
        for a in range(12):
            width = min(128, NLON - a * 128)
            cav = jnp.broadcast_to(ca[:, a : a + 1], (64, 128))
            sav = jnp.broadcast_to(sa[:, a : a + 1], (64, 128))
            f_ref[0, rows, a * 128 : a * 128 + width] = (cav * cb - sav * sb).astype(BF)[:, :width]
            f_ref[1, rows, a * 128 : a * 128 + width] = (-(sav * cb + cav * sb)).astype(BF)[:, :width]
        return carry

    lax.fori_loop(0, 8, long_rows, 0)

    k = lax.broadcasted_iota(jnp.int32, (MODES, 128), 0).astype(F32)
    degree = k + (m + 1.0)
    upper = jnp.sqrt((4.0 * degree * degree - 1.0) / (degree * degree - m * m))
    below = degree - 1.0
    lower = jnp.sqrt((below * below - m * m) / jnp.maximum(4.0 * below * below - 1.0, 1.0))
    up_ref[...] = upper
    low_ref[...] = upper * lower
    cosv = cosv_ref[...]
    start = 0.5 * (jnp.log(jnp.full((4, 128), m + 0.5, F32)) + logs_ref[order]) + m * logsin_ref[...]

    def block(b, carry):
        previous, current, scale = carry
        factor = jnp.exp(0.5 * scale)
        for offset in range(RENEW):
            step = b * RENEW + offset
            raw_ref[pl.ds(pl.multiple_of(step * 4, 4), 4), :] = current * factor * factor
            ua = jnp.broadcast_to(up_ref[pl.ds(step, 1), :], (4, 128)) * cosv
            lb = jnp.broadcast_to(low_ref[pl.ds(step, 1), :], (4, 128))
            previous, current = current, ua * current - lb * previous
        biggest = jnp.maximum(jnp.abs(previous), jnp.abs(current))
        shift = jnp.log(biggest)
        rescale = jnp.exp(-shift)
        return previous * rescale, current * rescale, scale + shift

    zero = jnp.zeros((4, 128), F32)
    lax.fori_loop(0, MODES // RENEW, block, (zero, zero + 1.0, start))
    live = lax.broadcasted_iota(jnp.int32, (MODES, 128), 0) < MODES - order
    for g in range(4):
        part = raw_ref[pl.ds(g, MODES, stride=4), :]
        part = jnp.where(live, part, 0.0) * math.sqrt(math.pi / NLAT)
        l_ref[:, g * 128 : (g + 1) * 128] = part.astype(BF)
        lt_ref[g * 128 : (g + 1) * 128, :] = jnp.transpose(part).astype(BF)


def tables(order_slots):
    theta = math.pi * (np.arange(NLAT) + 0.5) / NLAT
    cosv = jnp.asarray(np.cos(theta).reshape(4, 128), F32)
    logsin = jnp.asarray(np.log(np.sin(theta)).reshape(4, 128), F32)
    s = np.arange(1, MODES)
    logs = jnp.asarray(np.concatenate([[0.0], np.cumsum(np.log((2.0 * s - 1.0) / (2.0 * s)))]), F32)
    vm = pl.BlockSpec(memory_space=pltpu.VMEM)
    sm = pl.BlockSpec(memory_space=pltpu.SMEM)
    return pl.pallas_call(
        tables_kernel,
        out_shape=(
            jax.ShapeDtypeStruct((2, MODES, NLON), BF),
            jax.ShapeDtypeStruct((MODES, NLAT), BF),
            jax.ShapeDtypeStruct((NLAT, MODES), BF),
        ),
        in_specs=[sm, sm, vm, vm, vm],
        out_specs=(vm, vm, vm),
        scratch_shapes=[
            pltpu.VMEM((MODES, 128), F32),
            pltpu.VMEM((MODES, 128), F32),
            pltpu.VMEM((MODES * 4, 128), F32),
        ],
        compiler_params=pltpu.CompilerParams(vmem_limit_bytes=VMEM_BYTES),
        name="tables",
    )(order_slots, logs, order_slots.reshape(MODES, 1), cosv, logsin)


def pack_blocks(g0, g1, perm_ref, out_ref, stage_ref):
    for j in range(JL):
        cols = slice(j * CL, (j + 1) * CL)
        stage_ref[j] = jnp.concatenate([g0[:, cols], g1[:, cols]], axis=1).astype(BF)
    for g in range(4):
        rows = jnp.concatenate([stage_ref[j, g * 128 : (g + 1) * 128, :] for j in range(JL)], axis=0)
        out_ref[g * 32 : (g + 1) * 32] = dot(perm_ref[...], rows).astype(BF).reshape(32, 16, 128)


def unpack_blocks(r_ref, perm_ref, half, grid_ref):
    for g in range(4):
        rows = r_ref[g * 32 : (g + 1) * 32].reshape(512, 128)
        turned = dot(rows, perm_ref[...], TN)
        for j in range(JL):
            piece = turned[:, j * 128 : (j + 1) * 128]
            if half is not None:
                piece = piece * half[:, g * 128 : (g + 1) * 128]
            piece = piece.astype(BF)
            for r in range(2):
                grid_ref[r, j * CL : (j + 1) * CL, g * 128 : (g + 1) * 128] = piece[r * CL : (r + 1) * CL]


def first_kernel(x_ref, f_ref, sine_ref, perm_ref, out_ref, stage_ref):
    sines = sine_ref[...]
    g0 = dot(f_ref[0], x_ref[...], NT) * sines
    g1 = dot(f_ref[1], x_ref[...], NT) * sines
    pack_blocks(g0, g1, perm_ref, out_ref, stage_ref)


CHUNKS = ((0, 384), (384, 384), (768, 384), (1152, 288))


def middle_kernel(r_ref, x_ref, cot_ref, f_ref, halfrow_ref, halfcol_ref, perm_ref, y_ref, out_ref, grid_ref, slope_ref, stage_ref):
    unpack_blocks(r_ref, perm_ref, halfrow_ref[...], grid_ref)
    for first, width in CHUNKS:
        cols = slice(first, first + width)
        v = dot(grid_ref[0], f_ref[0, :, cols]) + dot(grid_ref[1], f_ref[1, :, cols])
        cdf = 0.5 * (1.0 + lax.erf(v * (1.0 / math.sqrt(2.0))))
        y_ref[:, cols] = (x_ref[:, cols].astype(F32) + v * cdf).astype(BF)
        slope = cdf + v * jnp.exp(-0.5 * v * v) * (1.0 / math.sqrt(2.0 * math.pi))
        slope_ref[:, cols] = (cot_ref[:, cols].astype(F32) * slope).astype(BF)
    hc = halfcol_ref[...]
    g0 = dot(f_ref[0], slope_ref[...], NT) * hc
    g1 = dot(f_ref[1], slope_ref[...], NT) * hc
    pack_blocks(g0, g1, perm_ref, out_ref, stage_ref)


def last_kernel(r_ref, cot_ref, f_ref, perm_ref, out_ref, grid_ref):
    unpack_blocks(r_ref, perm_ref, None, grid_ref)
    for first, width in CHUNKS:
        cols = slice(first, first + width)
        v = dot(grid_ref[0], f_ref[0, :, cols]) + dot(grid_ref[1], f_ref[1, :, cols])
        out_ref[:, cols] = (cot_ref[:, cols].astype(F32) + v).astype(BF)


def own_order(slots_ref):
    return slots_ref[lax.axis_index("lat") * NX + lax.axis_index("ch")]


def gain_rows(gain_ref, x, order):
    k = lax.broadcasted_iota(jnp.int32, (MODES, 128), 0)
    rolled = pltpu.roll(gain_ref[x], lax.rem(MODES - order, MODES), 0)
    return jnp.where(k < MODES - order, rolled, 0.0)


def forward_kernel(slots_ref, q_ref, l_ref, lt_ref, w_ref, gain_ref, coeff_ref, mixed_ref, spec_ref, ret_ref, flat_ref):
    order = own_order(slots_ref)
    values = jnp.concatenate([q_ref[x] for x in range(NX)], axis=1)
    coeff_ref[...] = dot(l_ref[...], values).astype(BF)
    mixed_ref[...] = dot(coeff_ref[...], w_ref[...]).astype(BF)
    for x in range(NX):
        cols = slice(x * 128, (x + 1) * 128)
        spec = mixed_ref[:, cols].astype(F32) * gain_rows(gain_ref, x, order)
        flat_ref[:, cols] = spec.astype(BF)
        spec_ref[x] = jnp.transpose(spec).astype(BF)
    ret = dot(lt_ref[...], flat_ref[...]).astype(BF)
    for x in range(NX):
        ret_ref[x] = ret[:, x * 128 : (x + 1) * 128]


def backward_kernel(slots_ref, q_ref, l_ref, lt_ref, w_ref, gain_ref, coeff_ref, mixed_ref, sine_ref, ret_ref, sums_ref, pre_ref):
    order = own_order(slots_ref)
    values = jnp.concatenate([q_ref[x] for x in range(NX)], axis=1)
    grad = dot(l_ref[...], values)
    for x in range(NX):
        cols = slice(x * 128, (x + 1) * 128)
        part = grad[:, cols]
        pre_ref[:, cols] = (part * gain_rows(gain_ref, x, order)).astype(BF)
        prod = pltpu.roll(part * mixed_ref[:, cols].astype(F32), order, 0)
        prod = prod[:, :CL] + prod[:, CL:]
        sums_ref[x, 128:384, :] = jnp.concatenate([prod[:256], prod[256:]], axis=1)
    mix = dot(coeff_ref[...], pre_ref[...], TN)
    for x in range(NX):
        blocks = []
        for i in range(NX):
            a = mix[i * 128 : i * 128 + CL, x * 128 : x * 128 + CL]
            b = mix[i * 128 + CL : (i + 1) * 128, x * 128 + CL : (x + 1) * 128]
            blocks.append(a + b)
        low = jnp.concatenate([blocks[0], blocks[1]], axis=0)
        high = jnp.concatenate([blocks[2], blocks[3]], axis=0)
        sums_ref[x, 0:128, :] = jnp.concatenate([low, high], axis=1)
    back = dot(pre_ref[...], w_ref[...], NT).astype(BF)
    ret = (dot(lt_ref[...], back) * sine_ref[...]).astype(BF)
    for x in range(NX):
        ret_ref[x] = ret[:, x * 128 : (x + 1) * 128]


class Place:
    def __init__(self):
        lat = lax.axis_index("lat")
        self.x = lax.axis_index("ch")
        self.c = lax.rem(lat, 2)
        self.y = lax.rem(lax.div(lat, 2), 8)
        self.z = lax.div(lat, 16)

    def at(self, z=None, y=None, c=None, x=None):
        z, y = (self.z if z is None else z), (self.y if y is None else y)
        c, x = (self.c if c is None else c), (self.x if x is None else x)
        return ((z * 8 + y) * 2 + c, x)


def around(value, step, count):
    return lax.rem(value + step, count)


def send(src, dst, ssem, rsem, target):
    pltpu.make_async_remote_copy(
        src_ref=src, dst_ref=dst, send_sem=ssem, recv_sem=rsem, device_id=target, device_id_type=MESH
    ).start()


def settle(view, sem):
    pltpu.make_async_copy(view, view, sem).wait()


def greet(me):
    barrier = pltpu.get_barrier_semaphore()
    other = 1 - me.c
    targets = [me.at(c=other)]
    for o in range(1, 8):
        targets += [me.at(y=around(me.y, o, 8)), me.at(z=around(me.z, o, 8))]
        targets += [me.at(y=around(me.y, o, 8), c=other), me.at(z=around(me.z, o, 8), c=other)]
    for o in range(1, 4):
        targets.append(me.at(x=around(me.x, o, 4)))
    for target in targets:
        pl.semaphore_signal(barrier, inc=1, device_id=target, device_id_type=MESH)
    pl.semaphore_wait(barrier, len(targets))


def lat_start(me, s_ref, ta_ref, tb_ref, ssem, rsem, lsem):
    pltpu.make_async_copy(s_ref.at[:, me.y, 0], ta_ref.at[me.y], lsem.at[0]).start()
    pltpu.make_async_copy(s_ref.at[me.z, :, 1], tb_ref.at[me.z], lsem.at[1]).start()
    for o in range(1, 8):
        y, z = around(me.y, o, 8), around(me.z, o, 8)
        send(s_ref.at[:, y, 0], ta_ref.at[me.y], ssem.at[0], rsem.at[0], me.at(y=y))
        send(s_ref.at[z, :, 1], tb_ref.at[me.z], ssem.at[1], rsem.at[1], me.at(z=z))


def lat_middle(me, ta_ref, tb_ref, r_ref, ssem, rsem, lsem):
    settle(ta_ref.at[0], lsem.at[0])
    settle(ta_ref.at[0:7], rsem.at[0])
    settle(tb_ref.at[0], lsem.at[1])
    settle(tb_ref.at[0:7], rsem.at[1])
    here_a, here_b = r_ref.at[me.z, :, me.c], r_ref.at[:, me.y, me.c]
    to_a, to_b = 2 + me.c, 3 - me.c
    for o in range(1, 8):
        y, z = around(me.y, o, 8), around(me.z, o, 8)
        send(ta_ref.at[:, z], here_a, ssem.at[to_a], rsem.at[to_a], me.at(z=z, c=0))
        send(tb_ref.at[:, y], here_b, ssem.at[to_b], rsem.at[to_b], me.at(y=y, c=1))

    @pl.when(me.c == 0)
    def _():
        pltpu.make_async_copy(ta_ref.at[:, me.z], here_a, lsem.at[2]).start()
        send(tb_ref.at[:, me.y], here_b, ssem.at[3], rsem.at[3], me.at(c=1))

    @pl.when(me.c == 1)
    def _():
        pltpu.make_async_copy(tb_ref.at[:, me.y], here_b, lsem.at[2]).start()
        send(ta_ref.at[:, me.z], here_a, ssem.at[3], rsem.at[3], me.at(c=0))


def lat_end(ta_ref, lsem, rsem):
    settle(ta_ref.at[0], lsem.at[2])
    settle(ta_ref.at[0:7], rsem.at[2])
    settle(ta_ref, rsem.at[3])


def lat_sent(ta_ref, ssem):
    settle(ta_ref.at[0:7], ssem.at[0])
    settle(ta_ref.at[0:7], ssem.at[1])
    settle(ta_ref.at[0:7], ssem.at[2])
    settle(ta_ref, ssem.at[3])


def x_start(me, src_ref, dst_ref, ssem, rsem, lsem):
    for o in (2, 1, 3):
        x = around(me.x, o, 4)
        send(src_ref.at[x], dst_ref.at[me.x], ssem, rsem, me.at(x=x))
    pltpu.make_async_copy(src_ref.at[me.x], dst_ref.at[me.x], lsem).start()


def x_end(dst_ref, rsem, lsem):
    settle(dst_ref.at[0], lsem)
    settle(dst_ref.at[0:3], rsem)


def to_orders_kernel(s_ref, perm_ref, q_ref, ta_ref, tb_ref, r_ref, p_ref, ssem, rsem, lsem):
    me = Place()
    greet(me)
    lat_start(me, s_ref, ta_ref, tb_ref, ssem, rsem, lsem)
    lat_middle(me, ta_ref, tb_ref, r_ref, ssem, rsem, lsem)
    lat_end(ta_ref, lsem, rsem)

    def turn(g, carry):
        rows = r_ref[g].reshape(256, 128)
        out = dot(perm_ref[...], rows).astype(BF)
        at = pl.ds(pl.multiple_of(g * 64, 64), 64)
        for s in range(4):
            p_ref[s, at, :] = out[s * 64 : (s + 1) * 64]
        return carry

    lax.fori_loop(0, 8, turn, 0)
    x_start(me, p_ref, q_ref, ssem.at[4], rsem.at[4], lsem.at[3])
    x_end(q_ref, rsem.at[4], lsem.at[3])
    lat_sent(ta_ref, ssem)
    settle(p_ref.at[0:3], ssem.at[4])


def spread(t_ref, perm_ref, s_ref):
    def turn(g, carry):
        at = pl.ds(pl.multiple_of(g * 64, 64), 64)
        rows = jnp.concatenate([t_ref[s, at, :] for s in range(4)], axis=0)
        s_ref[g] = dot(perm_ref[...], rows).astype(BF).reshape(8, 2, 16, 128)
        return carry

    lax.fori_loop(0, 8, turn, 0)


def to_grid_kernel(ret_ref, spec_ref, perm_ref, r_ref, out_ref, t_ref, s_ref, ta_ref, tb_ref, ssem, rsem, lsem):
    me = Place()
    greet(me)
    x_start(me, ret_ref, t_ref, ssem.at[4], rsem.at[4], lsem.at[3])
    x_start(me, spec_ref, out_ref, ssem.at[5], rsem.at[5], lsem.at[4])
    x_end(t_ref, rsem.at[4], lsem.at[3])
    spread(t_ref, perm_ref, s_ref)
    lat_start(me, s_ref, ta_ref, tb_ref, ssem, rsem, lsem)
    lat_middle(me, ta_ref, tb_ref, r_ref, ssem, rsem, lsem)
    lat_end(ta_ref, lsem, rsem)
    x_end(out_ref, rsem.at[5], lsem.at[4])
    lat_sent(ta_ref, ssem)
    settle(t_ref.at[0:3], ssem.at[4])
    settle(out_ref.at[0:3], ssem.at[5])


def to_grid_sums_kernel(
    ret_ref, sums_ref, perm_ref, r_ref, total_ref,
    t_ref, s_ref, ta_ref, tb_ref, v_ref, half_ref, core_ref, own_ref, ybuf_ref, piece_ref, zbuf_ref, fin_ref,
    ssem, rsem, lsem,
):
    me = Place()
    other = 1 - me.c
    greet(me)
    x_start(me, ret_ref, t_ref, ssem.at[4], rsem.at[4], lsem.at[3])
    x_start(me, sums_ref, v_ref, ssem.at[5], rsem.at[5], lsem.at[4])
    x_end(t_ref, rsem.at[4], lsem.at[3])
    spread(t_ref, perm_ref, s_ref)
    lat_start(me, s_ref, ta_ref, tb_ref, ssem, rsem, lsem)
    x_end(v_ref, rsem.at[5], lsem.at[4])
    half_ref[...] = ((v_ref[0] + v_ref[1]) + (v_ref[2] + v_ref[3])).reshape(2, 192, 128)
    send(half_ref.at[other], core_ref, ssem.at[6], rsem.at[6], me.at(c=other))
    lat_middle(me, ta_ref, tb_ref, r_ref, ssem, rsem, lsem)
    settle(core_ref, rsem.at[6])
    own_ref[...] = (half_ref[me.c] + core_ref[...]).reshape(8, 24, 128)
    for o in range(1, 8):
        y = around(me.y, o, 8)
        send(own_ref.at[y], ybuf_ref.at[me.y], ssem.at[7], rsem.at[7], me.at(y=y))
    ybuf_ref[me.y] = own_ref[me.y]
    settle(ybuf_ref.at[0:7], rsem.at[7])
    piece_ref[...] = jnp.sum(ybuf_ref[...], axis=0)
    for o in range(1, 8):
        z = around(me.z, o, 8)
        send(piece_ref, zbuf_ref.at[me.z], ssem.at[8], rsem.at[8], me.at(z=z))
    zbuf_ref[me.z] = piece_ref[...]
    settle(zbuf_ref.at[0:7], rsem.at[8])
    fin_ref[...] = jnp.sum(zbuf_ref[...], axis=0)
    for o in range(8):
        y = around(me.y, o, 8)
        if o > 0:
            send(fin_ref, total_ref.at[me.c, me.y], ssem.at[9], rsem.at[9], me.at(y=y))
        send(fin_ref, total_ref.at[me.c, me.y], ssem.at[10], rsem.at[10], me.at(y=y, c=other))
    total_ref[me.c, me.y] = fin_ref[...]
    lat_end(ta_ref, lsem, rsem)
    settle(total_ref.at[0, 0:7], rsem.at[9])
    settle(total_ref.at[0], rsem.at[10])
    lat_sent(ta_ref, ssem)
    settle(t_ref.at[0:3], ssem.at[4])
    settle(v_ref.at[0:3], ssem.at[5])
    settle(core_ref, ssem.at[6])
    settle(ybuf_ref.at[0:7], ssem.at[7])
    settle(zbuf_ref.at[0:7], ssem.at[8])
    settle(total_ref.at[0, 0:7], ssem.at[9])
    settle(total_ref.at[0], ssem.at[10])


VM = pl.BlockSpec(memory_space=pltpu.VMEM)
SM = pl.BlockSpec(memory_space=pltpu.SMEM)
BLOCKS = (NZ, NY, NC, 16, 128)


def local_call(kernel, outs, scratch, specs, name):
    return pl.pallas_call(
        kernel,
        out_shape=tuple(jax.ShapeDtypeStruct(*o) for o in outs),
        in_specs=specs,
        out_specs=tuple(VM for _ in outs),
        scratch_shapes=[pltpu.VMEM(*s) for s in scratch],
        compiler_params=pltpu.CompilerParams(vmem_limit_bytes=VMEM_BYTES),
        name=name,
    )


def exchange_call(kernel, outs, scratch, count, sems, ident, name):
    return pl.pallas_call(
        kernel,
        out_shape=tuple(jax.ShapeDtypeStruct(*o) for o in outs),
        in_specs=[VM] * count,
        out_specs=tuple(VM for _ in outs),
        scratch_shapes=[pltpu.VMEM(*s) for s in scratch]
        + [pltpu.SemaphoreType.DMA((sems,)), pltpu.SemaphoreType.DMA((sems,)), pltpu.SemaphoreType.DMA((5,))],
        compiler_params=pltpu.CompilerParams(vmem_limit_bytes=VMEM_BYTES, collective_id=ident, has_side_effects=True),
        name=name,
    )


def to_orders(blocks, perm, ident):
    (out,) = exchange_call(
        to_orders_kernel,
        [((NX, NLAT, 128), BF)],
        [((8, 8, 16, 128), BF), ((8, 8, 16, 128), BF), (BLOCKS, BF), ((4, 512, 128), BF)],
        2, 5, ident, "to_orders_%d" % ident,
    )(blocks.reshape(BLOCKS), perm)
    return out


def one_hot(rows):
    out = np.zeros((rows.size, rows.size), np.float32)
    out[np.arange(rows.size), rows] = 1.0
    return out


def body(grid_field, order_slots, mix_weight, degree_gain, cotangent):
    lat = lax.axis_index("lat")
    d, s, j = np.meshgrid(np.arange(32), np.arange(4), np.arange(4), indexing="ij")
    perm = jnp.asarray(one_hot((j * 128 + d * 4 + s).reshape(-1)), BF)
    s, e, j = np.meshgrid(np.arange(4), np.arange(16), np.arange(4), indexing="ij")
    turn = one_hot((e * 16 + s * 4 + j).reshape(-1))
    fore, back = jnp.asarray(turn, BF), jnp.asarray(turn.T, BF)
    sines = np.sin(math.pi * (np.arange(NLAT) + 0.5) / NLAT).astype(np.float32)
    band = lax.dynamic_slice_in_dim(jnp.asarray(sines), lat * JL, JL)
    band_row = jnp.repeat(band, CL).reshape(1, JL * CL)
    sine_col = jnp.asarray(sines).reshape(NLAT, 1)
    halving = jnp.where(order_slots == 0, 0.5, 1.0).astype(F32)
    x = jnp.transpose(grid_field, (1, 0, 2)).reshape(JL * CL, NLON)
    cot = jnp.transpose(cotangent, (1, 0, 2)).reshape(JL * CL, NLON)
    parts = mix_weight.reshape(NX, 1, CL, NX, 1, CL)
    same = jnp.asarray(np.eye(2).reshape(1, 2, 1, 1, 2, 1), BF)
    weights = (parts * same).reshape(512, 512)
    turned = jnp.transpose(degree_gain)
    gains = lax.all_gather(jnp.concatenate([turned, turned], axis=1), "ch", axis=0)

    f_tab, leg, leg_t = tables(order_slots)
    (blocks,) = local_call(
        first_kernel, [((128, 16, 128), BF)], [((4, 512, 128), BF)], [VM] * 4, "first"
    )(x, f_tab, band_row, perm)
    q = to_orders(blocks, fore, 0)
    coeffs, mixed, spec, ret = local_call(
        forward_kernel,
        [((512, 512), BF), ((512, 512), BF), ((4, 128, 512), BF), ((4, 512, 128), BF)],
        [((512, 512), BF)],
        [SM] + [VM] * 5,
        "forward",
    )(order_slots, q, leg, leg_t, weights, gains)
    received, spectrum = exchange_call(
        to_grid_kernel,
        [(BLOCKS, BF), ((4, 128, 512), BF)],
        [((4, 512, 128), BF), (BLOCKS, BF), ((8, 8, 16, 128), BF), ((8, 8, 16, 128), BF)],
        3, 6, 1, "to_grid_1",
    )(ret, spec, back)
    out, blocks = local_call(
        middle_kernel,
        [((256, NLON), BF), ((128, 16, 128), BF)],
        [((2, 256, 512), BF), ((256, NLON), BF), ((4, 512, 128), BF)],
        [VM] * 7,
        "middle",
    )(received.reshape(128, 16, 128), x, cot, f_tab, halving.reshape(1, 512), halving.reshape(512, 1), perm)
    q = to_orders(blocks, fore, 2)
    ret, sums = local_call(
        backward_kernel,
        [((4, 512, 128), BF), ((4, 384, 128), F32)],
        [((512, 512), BF)],
        [SM] + [VM] * 8,
        "backward",
    )(order_slots, q, leg, leg_t, weights, gains, coeffs, mixed, sine_col)
    received, total = exchange_call(
        to_grid_sums_kernel,
        [(BLOCKS, BF), ((2, 8, 24, 128), F32)],
        [
            ((4, 512, 128), BF), (BLOCKS, BF), ((8, 8, 16, 128), BF), ((8, 8, 16, 128), BF),
            ((4, 384, 128), F32), ((2, 192, 128), F32), ((192, 128), F32), ((8, 24, 128), F32),
            ((8, 24, 128), F32), ((24, 128), F32), ((8, 24, 128), F32), ((24, 128), F32),
        ],
        3, 11, 3, "to_grid_3",
    )(ret, sums, back)
    (grad,) = local_call(
        last_kernel, [((256, NLON), BF)], [((2, 256, 512), BF)], [VM] * 4, "last"
    )(received.reshape(128, 16, 128), cot, f_tab, perm)

    total = total.reshape(384, 128)
    mix = jnp.concatenate([total[:128, :CL], total[:128, CL:]], axis=0) / MODES
    gain = jnp.concatenate([total[128:, :CL], total[128:, CL:]], axis=0).T / math.sqrt(MODES)
    out = jnp.transpose(out.reshape(JL, CL, NLON), (1, 0, 2))
    grad = jnp.transpose(grad.reshape(JL, CL, NLON), (1, 0, 2))
    return out, spectrum.reshape(4, 2, CL, MODES), grad, mix, gain


def solution(mesh):
    placed = (P("ch", "lat", None), P(), P(), P("ch", None), P("ch", "lat", None))
    return jax.shard_map(
        body,
        mesh=mesh,
        in_specs=placed,
        out_specs=(
            P("ch", "lat", None),
            P("lat", None, "ch", None),
            P("ch", "lat", None),
            P(None, "ch"),
            P("ch", None),
        ),
        check_vma=False,
    )
```

```python
import math

import jax
import jax.numpy as jnp
import numpy as np
from jax import lax
from jax.experimental import pallas as pl
from jax.experimental.pallas import tpu as pltpu
from jax.sharding import PartitionSpec as P

MESH = pl.DeviceIdType.MESH
BF, F32 = jnp.bfloat16, jnp.float32
CL, JL, NLON = 64, 4, 1440
NZ, NY, NC, NX = 8, 8, 2, 4
NLAT, MODES = 512, 512
RENEW = 32
VMEM_BYTES = 56 * 1024 * 1024
NN = (((1,), (0,)), ((), ()))
NT = (((1,), (1,)), ((), ()))
TN = (((0,), (0,)), ((), ()))


def dot(a, b, dims=NN):
    return lax.dot_general(a, b, dims, preferred_element_type=F32)


def half_angle(steps):
    turns = jnp.floor(steps * (1.0 / NLON) + 0.5)
    t = (steps - turns * NLON) * (math.pi / NLON)
    u = t * t
    s = t * (1.0 + u * (-1.0 / 6 + u * (1.0 / 120 + u * (-1.0 / 5040 + u * (1.0 / 362880 + u * (-1.0 / 39916800))))))
    c = 1.0 + u * (-0.5 + u * (1.0 / 24 + u * (-1.0 / 720 + u * (1.0 / 40320 + u * (-1.0 / 3628800 + u * (1.0 / 479001600))))))
    return 1.0 - 2.0 * s * s, 2.0 * s * c


def long_tables(mcol_ref, f_ref):
    def long_rows(i, carry):
        rows = pl.ds(pl.multiple_of(i * 64, 64), 64)
        mc = mcol_ref[rows, :]
        lane = lax.broadcasted_iota(jnp.int32, (64, 128), 1).astype(F32)
        cb, sb = half_angle(mc * lane)
        ca, sa = half_angle(mc * (lane * 128.0))
        cb, sb = cb * math.sqrt(2.0 / NLON), sb * math.sqrt(2.0 / NLON)
        for a in range(12):
            width = min(128, NLON - a * 128)
            cav = jnp.broadcast_to(ca[:, a : a + 1], (64, 128))
            sav = jnp.broadcast_to(sa[:, a : a + 1], (64, 128))
            f_ref[0, rows, a * 128 : a * 128 + width] = (cav * cb - sav * sb).astype(BF)[:, :width]
            f_ref[1, rows, a * 128 : a * 128 + width] = (-(sav * cb + cav * sb)).astype(BF)[:, :width]
        return carry

    lax.fori_loop(0, 8, long_rows, 0)


def legendre_start(m, logs, logsin_ref, up_ref, low_ref):
    k = lax.broadcasted_iota(jnp.int32, (MODES, 128), 0).astype(F32)
    degree = k + (m + 1.0)
    upper = jnp.sqrt((4.0 * degree * degree - 1.0) / (degree * degree - m * m))
    below = degree - 1.0
    lower = jnp.sqrt((below * below - m * m) / jnp.maximum(4.0 * below * below - 1.0, 1.0))
    up_ref[...] = upper
    low_ref[...] = upper * lower
    start = 0.5 * (jnp.log(jnp.full((4, 128), m + 0.5, F32)) + logs) + m * logsin_ref[...]
    zero = jnp.zeros((4, 128), F32)
    return zero, zero + 1.0, start


def legendre_steps(first, last, carry, cosv, up_ref, low_ref, raw_ref):
    def block(b, carry):
        previous, current, scale = carry
        factor = jnp.exp(0.5 * scale)
        for offset in range(RENEW):
            step = b * RENEW + offset
            raw_ref[pl.ds(pl.multiple_of(step * 4, 4), 4), :] = current * factor * factor
            ua = jnp.broadcast_to(up_ref[pl.ds(step, 1), :], (4, 128)) * cosv
            lb = jnp.broadcast_to(low_ref[pl.ds(step, 1), :], (4, 128))
            previous, current = current, ua * current - lb * previous
        biggest = jnp.maximum(jnp.abs(previous), jnp.abs(current))
        shift = jnp.log(biggest)
        rescale = jnp.exp(-shift)
        return previous * rescale, current * rescale, scale + shift

    return lax.fori_loop(first, last, block, carry)


def legendre_end(order, raw_ref, l_ref, lt_ref, shift_ref):
    live = lax.broadcasted_iota(jnp.int32, (MODES, 128), 0) < MODES - order
    for g in range(4):
        part = raw_ref[pl.ds(g, MODES, stride=4), :]
        part = jnp.where(live, part, 0.0) * math.sqrt(math.pi / NLAT)
        l_ref[:, g * 128 : (g + 1) * 128] = part.astype(BF)
        lt_ref[g * 128 : (g + 1) * 128, :] = jnp.transpose(part).astype(BF)
    k = lax.broadcasted_iota(jnp.int32, (MODES, MODES), 0)
    l = lax.broadcasted_iota(jnp.int32, (MODES, MODES), 1)
    shift_ref[...] = jnp.where(l - k == order, 1.0, 0.0).astype(BF)


def pack_blocks(g0, g1, perm_ref, s_ref, stage_ref):
    for j in range(JL):
        cols = slice(j * CL, (j + 1) * CL)
        stage_ref[j] = jnp.concatenate([g0[:, cols], g1[:, cols]], axis=1).astype(BF)
    for g in range(4):
        rows = jnp.concatenate([stage_ref[j, g * 128 : (g + 1) * 128, :] for j in range(JL)], axis=0)
        s_ref[2 * g : 2 * g + 2] = dot(perm_ref[...], rows).astype(BF).reshape(2, 8, 2, 16, 128)


def unpack_blocks(r_ref, perm_ref, half, grid_ref):
    for g in range(4):
        rows = r_ref[2 * g : 2 * g + 2].reshape(512, 128)
        turned = dot(rows, perm_ref[...], TN)
        for j in range(JL):
            piece = turned[:, j * 128 : (j + 1) * 128]
            if half is not None:
                piece = piece * half[:, g * 128 : (g + 1) * 128]
            piece = piece.astype(BF)
            for r in range(2):
                grid_ref[r, j * CL : (j + 1) * CL, g * 128 : (g + 1) * 128] = piece[r * CL : (r + 1) * CL]


CHUNKS = ((0, 384), (384, 384), (768, 384), (1152, 288))


def middle(grid_ref, x_ref, cot_ref, f_ref, y_ref, slope_ref):
    for first, width in CHUNKS:
        cols = slice(first, first + width)
        v = dot(grid_ref[0], f_ref[0, :, cols]) + dot(grid_ref[1], f_ref[1, :, cols])
        cdf = 0.5 * (1.0 + lax.erf(v * (1.0 / math.sqrt(2.0))))
        y_ref[:, cols] = (x_ref[:, cols].astype(F32) + v * cdf).astype(BF)
        slope = cdf + v * jnp.exp(-0.5 * v * v) * (1.0 / math.sqrt(2.0 * math.pi))
        slope_ref[:, cols] = (cot_ref[:, cols].astype(F32) * slope).astype(BF)


def last(grid_ref, cot_ref, f_ref, out_ref):
    for first, width in CHUNKS:
        cols = slice(first, first + width)
        v = dot(grid_ref[0], f_ref[0, :, cols]) + dot(grid_ref[1], f_ref[1, :, cols])
        out_ref[:, cols] = (cot_ref[:, cols].astype(F32) + v).astype(BF)


def mixing_weights(w_ref, w2_ref):
    zero = jnp.zeros((CL, CL), F32)
    for x in range(NX):
        slab = w_ref[x * CL : (x + 1) * CL, :].astype(F32)
        pieces = [slab[:, i * CL : (i + 1) * CL] for i in range(NX)]
        top = jnp.concatenate([a for p in pieces for a in (p, zero)], axis=1)
        low = jnp.concatenate([a for p in pieces for a in (zero, p)], axis=1)
        w2_ref[x * 128 : x * 128 + CL, :] = top.astype(BF)
        w2_ref[x * 128 + CL : (x + 1) * 128, :] = low.astype(BF)


def split_gain(gain_ref, out_ref):
    turned = jnp.transpose(gain_ref[...])
    high = turned.astype(BF).astype(F32)
    out_ref[...] = jnp.concatenate([high, turned - high], axis=1).astype(BF)


def gain_rows(shift_ref, garr_ref, rows_ref):
    for x in range(NX):
        both = dot(shift_ref[...], garr_ref[x])
        row = both[:, :CL] + both[:, CL:]
        rows_ref[:, x * 128 : (x + 1) * 128] = jnp.concatenate([row, row], axis=1)


def gain_sums(grad_ref, mixed_ref, shift_ref, sums_ref):
    for x in range(NX):
        cols = slice(x * 128, (x + 1) * 128)
        prod = grad_ref[:, cols] * mixed_ref[:, cols].astype(F32)
        prod = prod[:, :CL] + prod[:, CL:]
        high = prod.astype(BF).astype(F32)
        both = dot(shift_ref[...], jnp.concatenate([high, prod - high], axis=1).astype(BF), TN)
        both = both[:, :CL] + both[:, CL:]
        sums_ref[x, 128:384, :] = jnp.concatenate([both[:256], both[256:]], axis=1)


def mix_sums(coeff_ref, pre_ref, sums_ref):
    mix = dot(coeff_ref[...], pre_ref[...], TN)
    for x in range(NX):
        blocks = []
        for i in range(NX):
            a = mix[i * 128 : i * 128 + CL, x * 128 : x * 128 + CL]
            b = mix[i * 128 + CL : (i + 1) * 128, x * 128 + CL : (x + 1) * 128]
            blocks.append(a + b)
        low = jnp.concatenate([blocks[0], blocks[1]], axis=0)
        high = jnp.concatenate([blocks[2], blocks[3]], axis=0)
        sums_ref[x, 0:128, :] = jnp.concatenate([low, high], axis=1)


def flat(q_ref):
    return jnp.concatenate([q_ref[x] for x in range(NX)], axis=1)


def split_lanes(value, ref):
    for x in range(NX):
        ref[x] = value[:, x * 128 : (x + 1) * 128]


class Place:
    def __init__(self):
        lat = lax.axis_index("lat")
        self.x = lax.axis_index("ch")
        self.c = lax.rem(lat, 2)
        self.y = lax.rem(lax.div(lat, 2), 8)
        self.z = lax.div(lat, 16)

    def at(self, z=None, y=None, c=None, x=None):
        z, y = (self.z if z is None else z), (self.y if y is None else y)
        c, x = (self.c if c is None else c), (self.x if x is None else x)
        return ((z * 8 + y) * 2 + c, x)


def around(value, step, count):
    return lax.rem(value + step, count)


def send(src, dst, ssem, rsem, target):
    pltpu.make_async_remote_copy(
        src_ref=src, dst_ref=dst, send_sem=ssem, recv_sem=rsem, device_id=target, device_id_type=MESH
    ).start()


def settle(view, sem):
    pltpu.make_async_copy(view, view, sem).wait()


def greet(me):
    barrier = pltpu.get_barrier_semaphore()
    other = 1 - me.c
    targets = [me.at(c=other)]
    for o in range(1, 8):
        targets += [me.at(y=around(me.y, o, 8)), me.at(z=around(me.z, o, 8))]
        targets += [me.at(y=around(me.y, o, 8), c=other), me.at(z=around(me.z, o, 8), c=other)]
    for o in range(1, 4):
        targets.append(me.at(x=around(me.x, o, 4)))
    for target in targets:
        pl.semaphore_signal(barrier, inc=1, device_id=target, device_id_type=MESH)
    return len(targets)


def lat_start(me, s_ref, ta_ref, tb_ref, ssem, rsem, lsem):
    pltpu.make_async_copy(s_ref.at[:, me.y, 0], ta_ref.at[me.y], lsem.at[0]).start()
    pltpu.make_async_copy(s_ref.at[me.z, :, 1], tb_ref.at[me.z], lsem.at[1]).start()
    for o in range(1, 8):
        y, z = around(me.y, o, 8), around(me.z, o, 8)
        send(s_ref.at[:, y, 0], ta_ref.at[me.y], ssem.at[0], rsem.at[0], me.at(y=y))
        send(s_ref.at[z, :, 1], tb_ref.at[me.z], ssem.at[1], rsem.at[1], me.at(z=z))


def lat_middle(me, ta_ref, tb_ref, r_ref, ssem, rsem, lsem):
    settle(ta_ref.at[0], lsem.at[0])
    settle(ta_ref.at[0:7], rsem.at[0])
    settle(tb_ref.at[0], lsem.at[1])
    settle(tb_ref.at[0:7], rsem.at[1])
    here_a, here_b = r_ref.at[me.z, :, me.c], r_ref.at[:, me.y, me.c]
    to_a, to_b = 2 + me.c, 3 - me.c
    for o in range(1, 8):
        y, z = around(me.y, o, 8), around(me.z, o, 8)
        send(ta_ref.at[:, z], here_a, ssem.at[to_a], rsem.at[to_a], me.at(z=z, c=0))
        send(tb_ref.at[:, y], here_b, ssem.at[to_b], rsem.at[to_b], me.at(y=y, c=1))

    @pl.when(me.c == 0)
    def _():
        pltpu.make_async_copy(ta_ref.at[:, me.z], here_a, lsem.at[2]).start()
        send(tb_ref.at[:, me.y], here_b, ssem.at[3], rsem.at[3], me.at(c=1))

    @pl.when(me.c == 1)
    def _():
        pltpu.make_async_copy(tb_ref.at[:, me.y], here_b, lsem.at[2]).start()
        send(ta_ref.at[:, me.z], here_a, ssem.at[3], rsem.at[3], me.at(c=0))


def lat_end(ta_ref, lsem, rsem):
    settle(ta_ref.at[0], lsem.at[2])
    settle(ta_ref.at[0:7], rsem.at[2])
    settle(ta_ref, rsem.at[3])


def lat_sent(ta_ref, ssem):
    settle(ta_ref.at[0:7], ssem.at[0])
    settle(ta_ref.at[0:7], ssem.at[1])
    settle(ta_ref.at[0:7], ssem.at[2])
    settle(ta_ref, ssem.at[3])


def x_start(me, src_ref, dst_ref, ssem, rsem, lsem):
    for o in (2, 1, 3):
        x = around(me.x, o, 4)
        send(src_ref.at[x], dst_ref.at[me.x], ssem, rsem, me.at(x=x))
    pltpu.make_async_copy(src_ref.at[me.x], dst_ref.at[me.x], lsem).start()


def x_end(dst_ref, rsem, lsem):
    settle(dst_ref.at[0], lsem)
    settle(dst_ref.at[0:3], rsem)


def turn_blocks(r_ref, perm_ref, p_ref):
    def turn(g, carry):
        rows = r_ref[g].reshape(256, 128)
        out = dot(perm_ref[...], rows).astype(BF)
        at = pl.ds(pl.multiple_of(g * 64, 64), 64)
        for s in range(4):
            p_ref[s, at, :] = out[s * 64 : (s + 1) * 64]
        return carry

    lax.fori_loop(0, 8, turn, 0)


def spread(t_ref, perm_ref, s_ref):
    def turn(g, carry):
        at = pl.ds(pl.multiple_of(g * 64, 64), 64)
        rows = jnp.concatenate([t_ref[s, at, :] for s in range(4)], axis=0)
        s_ref[g] = dot(perm_ref[...], rows, TN).astype(BF).reshape(8, 2, 16, 128)
        return carry

    lax.fori_loop(0, 8, turn, 0)


def whole_kernel(
    slots_ref, logs_ref, mrow_ref, cosv_ref, logsin_ref, band_ref, sine_ref, perm_ref, turn_ref, w_ref, gain_ref, x_ref, cot_ref,
    y_ref, spectrum_ref, out_ref, mix_ref, ggain_ref,
    f_ref, mcol_ref, up_ref, low_ref, raw_ref, l_ref, lt_ref, shift_ref, w2_ref, gsend_ref, garr_ref, grows_ref,
    stage_ref, grid_ref, slope_ref, coeff_ref, mixed_ref, flat_ref, pre_ref, grad_ref, spec_ref, ret_ref, ret2_ref,
    s_refs, ta_refs, tb_refs, r_refs, p_refs, q_refs,
    sums_ref, v_ref, half_ref, core_ref, own_ref, ybuf_ref, piece_ref, zbuf_ref, fin_ref, total_ref,
    ssem, rsem, lsem, xs, xr, xl, gs, gr,
):
    me = Place()
    other = 1 - me.c
    peers = greet(me)
    lat = lax.axis_index("lat")
    order = slots_ref[lat * NX + me.x]
    m = order.astype(F32)
    mrow = mrow_ref[...]
    half_row = jnp.where(mrow == 0, 0.5, 1.0)
    mcol_ref[...] = jnp.transpose(jnp.broadcast_to(mrow.astype(F32), (128, MODES)))
    split_gain(gain_ref, gsend_ref)
    long_tables(mcol_ref, f_ref)

    sines = band_ref[pl.ds(lat, 1), :]
    g0 = dot(f_ref[0], x_ref[...], NT) * sines
    g1 = dot(f_ref[1], x_ref[...], NT) * sines
    pack_blocks(g0, g1, perm_ref, s_refs.at[0], stage_ref)
    pl.semaphore_wait(pltpu.get_barrier_semaphore(), peers)

    def links(i):
        return ssem.at[i], rsem.at[i], lsem.at[i]

    def xlinks(i):
        return xs.at[i], xr.at[i], xl.at[i]

    def begin(i):
        lat_start(me, s_refs.at[i], ta_refs.at[i], tb_refs.at[i], *links(i))

    def carry_on(i):
        lat_middle(me, ta_refs.at[i], tb_refs.at[i], r_refs.at[i], *links(i))

    def finish(i):
        lat_end(ta_refs.at[i], lsem.at[i], rsem.at[i])

    begin(0)
    for o in range(1, 4):
        x = around(me.x, o, 4)
        send(gsend_ref, garr_ref.at[me.x], xs.at[6], xr.at[6], me.at(x=x))
    garr_ref[me.x] = gsend_ref[...]
    mixing_weights(w_ref, w2_ref)
    carry = legendre_start(m, logs_ref[order], logsin_ref, up_ref, low_ref)
    cosv = cosv_ref[...]
    carry = legendre_steps(0, 6, carry, cosv, up_ref, low_ref, raw_ref)
    carry_on(0)
    legendre_steps(6, MODES // RENEW, carry, cosv, up_ref, low_ref, raw_ref)
    legendre_end(order, raw_ref, l_ref, lt_ref, shift_ref)
    finish(0)
    turn_blocks(r_refs.at[0], turn_ref, p_refs.at[0])
    x_start(me, p_refs.at[0], q_refs.at[0], *xlinks(0))
    settle(garr_ref.at[0:3], xr.at[6])
    gain_rows(shift_ref, garr_ref, grows_ref)
    x_end(q_refs.at[0], xr.at[0], xl.at[0])

    coeff_ref[...] = dot(l_ref[...], flat(q_refs.at[0])).astype(BF)
    mixed_ref[...] = dot(coeff_ref[...], w2_ref[...]).astype(BF)
    flat_ref[...] = (mixed_ref[...].astype(F32) * grows_ref[...]).astype(BF)
    split_lanes(dot(lt_ref[...], flat_ref[...]).astype(BF), ret_ref)
    x_start(me, ret_ref, p_refs.at[1], *xlinks(1))
    for x in range(NX):
        spec_ref[x] = jnp.transpose(flat_ref[:, x * 128 : (x + 1) * 128].astype(F32)).astype(BF)
    x_start(me, spec_ref, spectrum_ref, *xlinks(2))
    x_end(p_refs.at[1], xr.at[1], xl.at[1])
    spread(p_refs.at[1], turn_ref, s_refs.at[1])
    begin(1)
    carry_on(1)
    finish(1)

    unpack_blocks(r_refs.at[1], perm_ref, half_row, grid_ref)
    middle(grid_ref, x_ref, cot_ref, f_ref, y_ref, slope_ref)
    mcol = mcol_ref[...]
    half_col = jnp.where(jnp.concatenate([mcol, mcol], axis=1) == 0.0, 0.5, 1.0)
    g0 = dot(f_ref[0], slope_ref[...], NT) * half_col
    g1 = dot(f_ref[1], slope_ref[...], NT) * half_col
    pack_blocks(g0, g1, perm_ref, s_refs.at[2], stage_ref)
    begin(2)
    carry_on(2)
    finish(2)
    turn_blocks(r_refs.at[2], turn_ref, p_refs.at[2])
    x_start(me, p_refs.at[2], q_refs.at[1], *xlinks(3))
    x_end(q_refs.at[1], xr.at[3], xl.at[3])

    grad_ref[...] = dot(l_ref[...], flat(q_refs.at[1]))
    pre_ref[...] = (grad_ref[...] * grows_ref[...]).astype(BF)
    back = dot(pre_ref[...], w2_ref[...], NT).astype(BF)
    split_lanes((dot(lt_ref[...], back) * sine_ref[...]).astype(BF), ret2_ref)
    x_start(me, ret2_ref, p_refs.at[3], *xlinks(4))
    gain_sums(grad_ref, mixed_ref, shift_ref, sums_ref)
    mix_sums(coeff_ref, pre_ref, sums_ref)
    x_start(me, sums_ref, v_ref, *xlinks(5))
    x_end(p_refs.at[3], xr.at[4], xl.at[4])
    spread(p_refs.at[3], turn_ref, s_refs.at[3])
    begin(3)
    x_end(v_ref, xr.at[5], xl.at[5])
    half_ref[...] = ((v_ref[0] + v_ref[1]) + (v_ref[2] + v_ref[3])).reshape(2, 192, 128)
    send(half_ref.at[other], core_ref, gs.at[0], gr.at[0], me.at(c=other))
    carry_on(3)
    settle(core_ref, gr.at[0])
    own_ref[...] = (half_ref[me.c] + core_ref[...]).reshape(8, 24, 128)
    for o in range(1, 8):
        y = around(me.y, o, 8)
        send(own_ref.at[y], ybuf_ref.at[me.y], gs.at[1], gr.at[1], me.at(y=y))
    ybuf_ref[me.y] = own_ref[me.y]
    settle(ybuf_ref.at[0:7], gr.at[1])
    piece_ref[...] = jnp.sum(ybuf_ref[...], axis=0)
    for o in range(1, 8):
        z = around(me.z, o, 8)
        send(piece_ref, zbuf_ref.at[me.z], gs.at[2], gr.at[2], me.at(z=z))
    zbuf_ref[me.z] = piece_ref[...]
    settle(zbuf_ref.at[0:7], gr.at[2])
    fin_ref[...] = jnp.sum(zbuf_ref[...], axis=0)
    for o in range(8):
        y = around(me.y, o, 8)
        if o > 0:
            send(fin_ref, total_ref.at[me.c, me.y], gs.at[3], gr.at[3], me.at(y=y))
        send(fin_ref, total_ref.at[me.c, me.y], gs.at[4], gr.at[4], me.at(y=y, c=other))
    total_ref[me.c, me.y] = fin_ref[...]
    finish(3)

    unpack_blocks(r_refs.at[3], perm_ref, None, grid_ref)
    last(grid_ref, cot_ref, f_ref, out_ref)
    settle(total_ref.at[0, 0:7], gr.at[3])
    settle(total_ref.at[0], gr.at[4])
    mix = total_ref[0].reshape(192, 128)[0:128] * (1.0 / MODES)
    mix_ref[...] = jnp.concatenate([mix[:, :CL], mix[:, CL:]], axis=0)
    gain = jnp.concatenate([total_ref[0].reshape(192, 128)[128:192], total_ref[1].reshape(192, 128)], axis=0)
    gain = jnp.concatenate([gain[:, :CL], gain[:, CL:]], axis=0) * (1.0 / math.sqrt(MODES))
    ggain_ref[...] = jnp.transpose(gain)

    for i in range(4):
        lat_sent(ta_refs.at[i], ssem.at[i])
    x_end(spectrum_ref, xr.at[2], xl.at[2])
    for i in range(5):
        settle(p_refs.at[0, 0:3], xs.at[i])
    settle(v_ref.at[0:3], xs.at[5])
    settle(garr_ref.at[0:3], xs.at[6])
    settle(core_ref, gs.at[0])
    settle(ybuf_ref.at[0:7], gs.at[1])
    settle(zbuf_ref.at[0:7], gs.at[2])
    settle(total_ref.at[0, 0:7], gs.at[3])
    settle(total_ref.at[0], gs.at[4])


VM = pl.BlockSpec(memory_space=pltpu.VMEM)
SM = pl.BlockSpec(memory_space=pltpu.SMEM)


def whole(*operands):
    scratch = [
        ((2, MODES, NLON), BF), ((MODES, 128), F32), ((MODES, 128), F32), ((MODES, 128), F32), ((MODES * 4, 128), F32),
        ((512, 512), BF), ((512, 512), BF), ((512, 512), BF), ((512, 512), BF), ((512, 128), BF), ((4, 512, 128), BF),
        ((512, 512), F32),
        ((4, 512, 128), BF), ((2, 256, 512), BF), ((256, NLON), BF), ((512, 512), BF), ((512, 512), BF), ((512, 512), BF),
        ((512, 512), BF), ((512, 512), F32), ((4, 128, 512), BF), ((4, 512, 128), BF), ((4, 512, 128), BF),
        ((4, NZ, NY, NC, 16, 128), BF), ((4, 8, 8, 16, 128), BF), ((4, 8, 8, 16, 128), BF), ((4, NZ, NY, NC, 16, 128), BF),
        ((4, 4, 512, 128), BF), ((2, 4, 512, 128), BF),
        ((4, 384, 128), F32), ((4, 384, 128), F32), ((2, 192, 128), F32), ((192, 128), F32), ((8, 24, 128), F32),
        ((8, 24, 128), F32), ((24, 128), F32), ((8, 24, 128), F32), ((24, 128), F32), ((2, 8, 24, 128), F32),
    ]
    sems = [(4, 4), (4, 4), (4, 3), (7,), (7,), (7,), (5,), (5,)]
    outs = [((256, NLON), BF), ((4, 128, 512), BF), ((256, NLON), BF), ((256, 64), F32), ((64, 512), F32)]
    return pl.pallas_call(
        whole_kernel,
        out_shape=tuple(jax.ShapeDtypeStruct(*o) for o in outs),
        in_specs=[SM, SM] + [VM] * (len(operands) - 2),
        out_specs=tuple(VM for _ in outs),
        scratch_shapes=[pltpu.VMEM(*s) for s in scratch] + [pltpu.SemaphoreType.DMA(s) for s in sems],
        compiler_params=pltpu.CompilerParams(vmem_limit_bytes=VMEM_BYTES, collective_id=0, has_side_effects=True),
        name="whole",
    )(*operands)


def one_hot(rows):
    out = np.zeros((rows.size, rows.size), np.float32)
    out[np.arange(rows.size), rows] = 1.0
    return jnp.asarray(out, BF)


def body(grid_field, order_slots, mix_weight, degree_gain, cotangent):
    d, s, j = np.meshgrid(np.arange(32), np.arange(4), np.arange(4), indexing="ij")
    perm = one_hot((j * 128 + d * 4 + s).reshape(-1))
    s, e, j = np.meshgrid(np.arange(4), np.arange(16), np.arange(4), indexing="ij")
    turn = one_hot((e * 16 + s * 4 + j).reshape(-1))
    theta = math.pi * (np.arange(NLAT) + 0.5) / NLAT
    cosv = jnp.asarray(np.cos(theta).reshape(4, 128), F32)
    logsin = jnp.asarray(np.log(np.sin(theta)).reshape(4, 128), F32)
    band = jnp.asarray(np.repeat(np.sin(theta).reshape(128, JL), CL, axis=1), F32)
    sine_col = jnp.asarray(np.repeat(np.sin(theta).reshape(NLAT, 1), 512, axis=1), F32)
    n = np.arange(1, MODES)
    logs = jnp.asarray(np.concatenate([[0.0], np.cumsum(np.log((2.0 * n - 1.0) / (2.0 * n)))]), F32)
    x = jnp.transpose(grid_field, (1, 0, 2)).reshape(JL * CL, NLON)
    cot = jnp.transpose(cotangent, (1, 0, 2)).reshape(JL * CL, NLON)
    out, spectrum, grad, mix, gain = whole(
        order_slots, logs, order_slots.reshape(1, MODES), cosv, logsin, band, sine_col, perm, turn, mix_weight, degree_gain, x, cot
    )
    out = jnp.transpose(out.reshape(JL, CL, NLON), (1, 0, 2))
    grad = jnp.transpose(grad.reshape(JL, CL, NLON), (1, 0, 2))
    return out, spectrum.reshape(4, 2, CL, MODES), grad, mix, gain


def solution(mesh):
    placed = (P("ch", "lat", None), P(), P(), P("ch", None), P("ch", "lat", None))
    return jax.shard_map(
        body,
        mesh=mesh,
        in_specs=placed,
        out_specs=(
            P("ch", "lat", None),
            P("lat", None, "ch", None),
            P("ch", "lat", None),
            P(None, "ch"),
            P("ch", None),
        ),
        check_vma=False,
    )
```

```python
import math

import jax
import jax.numpy as jnp
import numpy as np
from jax import lax
from jax.experimental import pallas as pl
from jax.experimental.pallas import tpu as pltpu
from jax.sharding import PartitionSpec as P

MESH = pl.DeviceIdType.MESH
BF, F32 = jnp.bfloat16, jnp.float32
CL, JL, NLON = 64, 4, 1440
NZ, NY, NC, NX = 8, 8, 2, 4
NLAT, MODES = 512, 512
RENEW = 32
VMEM_BYTES = 56 * 1024 * 1024
NN = (((1,), (0,)), ((), ()))
NT = (((1,), (1,)), ((), ()))
TN = (((0,), (0,)), ((), ()))


def dot(a, b, dims=NN):
    return lax.dot_general(a, b, dims, preferred_element_type=F32)


def half_angle(steps):
    turns = jnp.floor(steps * (1.0 / NLON) + 0.5)
    t = (steps - turns * NLON) * (math.pi / NLON)
    u = t * t
    s = t * (1.0 + u * (-1.0 / 6 + u * (1.0 / 120 + u * (-1.0 / 5040 + u * (1.0 / 362880 + u * (-1.0 / 39916800))))))
    c = 1.0 + u * (-0.5 + u * (1.0 / 24 + u * (-1.0 / 720 + u * (1.0 / 40320 + u * (-1.0 / 3628800 + u * (1.0 / 479001600))))))
    return 1.0 - 2.0 * s * s, 2.0 * s * c


def long_tables(mcol_ref, f_ref):
    def long_rows(i, carry):
        rows = pl.ds(pl.multiple_of(i * 64, 64), 64)
        lower = pl.ds(pl.multiple_of(i * 64 + MODES, 64), 64)
        mc = mcol_ref[rows, :]
        lane = lax.broadcasted_iota(jnp.int32, (64, 128), 1).astype(F32)
        cb, sb = half_angle(mc * lane)
        ca, sa = half_angle(mc * (lane * 128.0))
        cb, sb = cb * math.sqrt(2.0 / NLON), sb * math.sqrt(2.0 / NLON)
        for a in range(12):
            width = min(128, NLON - a * 128)
            cav = jnp.broadcast_to(ca[:, a : a + 1], (64, 128))
            sav = jnp.broadcast_to(sa[:, a : a + 1], (64, 128))
            f_ref[rows, a * 128 : a * 128 + width] = (cav * cb - sav * sb).astype(BF)[:, :width]
            f_ref[lower, a * 128 : a * 128 + width] = (-(sav * cb + cav * sb)).astype(BF)[:, :width]
        return carry

    lax.fori_loop(0, 8, long_rows, 0)


def legendre_start(m, logs, logsin, up_ref, low_ref):
    k = lax.broadcasted_iota(jnp.int32, (MODES, 128), 0).astype(F32)
    degree = k + (m + 1.0)
    upper = jnp.sqrt((4.0 * degree * degree - 1.0) / (degree * degree - m * m))
    below = degree - 1.0
    lower = jnp.sqrt((below * below - m * m) / jnp.maximum(4.0 * below * below - 1.0, 1.0))
    up_ref[...] = upper
    low_ref[...] = upper * lower
    start = 0.5 * (jnp.log(jnp.full((4, 128), m + 0.5, F32)) + logs) + m * logsin
    zero = jnp.zeros((4, 128), F32)
    return zero, zero + 1.0, start


def legendre_steps(first, last, carry, cosv, up_ref, low_ref, raw_ref):
    def block(b, carry):
        previous, current, scale = carry
        factor = jnp.exp(0.5 * scale)
        for offset in range(RENEW):
            step = b * RENEW + offset
            raw_ref[pl.ds(pl.multiple_of(step * 4, 4), 4), :] = current * factor * factor
            ua = jnp.broadcast_to(up_ref[pl.ds(step, 1), :], (4, 128)) * cosv
            lb = jnp.broadcast_to(low_ref[pl.ds(step, 1), :], (4, 128))
            previous, current = current, ua * current - lb * previous
        biggest = jnp.maximum(jnp.abs(previous), jnp.abs(current))
        shift = jnp.log(biggest)
        rescale = jnp.exp(-shift)
        return previous * rescale, current * rescale, scale + shift

    return lax.fori_loop(first, last, block, carry)


def legendre_end(order, raw_ref, l_ref, lt_ref, shift_ref, shift_t_ref):
    live = lax.broadcasted_iota(jnp.int32, (MODES, 128), 0) < MODES - order
    for g in range(4):
        part = raw_ref[pl.ds(g, MODES, stride=4), :]
        part = jnp.where(live, part, 0.0) * math.sqrt(math.pi / NLAT)
        l_ref[:, g * 128 : (g + 1) * 128] = part.astype(BF)
        lt_ref[g * 128 : (g + 1) * 128, :] = jnp.transpose(part).astype(BF)
    k = lax.broadcasted_iota(jnp.int32, (MODES, MODES), 0)
    l = lax.broadcasted_iota(jnp.int32, (MODES, MODES), 1)
    shift_ref[...] = jnp.where(l - k == order, 1.0, 0.0).astype(BF)
    shift_t_ref[...] = jnp.where(k - l == order, 1.0, 0.0).astype(BF)


def pack_blocks(g, perm_ref, s_ref, stage_ref):
    for j in range(JL):
        cols = slice(j * CL, (j + 1) * CL)
        stage_ref[j] = jnp.concatenate([g[:MODES, cols], g[MODES:, cols]], axis=1).astype(BF)
    for g in range(4):
        rows = jnp.concatenate([stage_ref[j, g * 128 : (g + 1) * 128, :] for j in range(JL)], axis=0)
        s_ref[2 * g : 2 * g + 2] = dot(perm_ref[...], rows).astype(BF).reshape(2, 8, 2, 16, 128)


def unpack_blocks(r_ref, perm_ref, half, grid_ref):
    for g in range(4):
        rows = r_ref[2 * g : 2 * g + 2].reshape(512, 128)
        turned = dot(rows, perm_ref[...], TN)
        for j in range(JL):
            piece = turned[:, j * 128 : (j + 1) * 128]
            if half is not None:
                piece = piece * half[:, g * 128 : (g + 1) * 128]
            piece = piece.astype(BF)
            for r in range(2):
                at = r * MODES + g * 128
                grid_ref[j * CL : (j + 1) * CL, at : at + 128] = piece[r * CL : (r + 1) * CL]


CHUNKS = ((0, 384), (384, 384), (768, 384), (1152, 288))


def to_rows(field_ref, rows_ref):
    for j in range(JL):
        rows_ref[j * CL : (j + 1) * CL, :] = field_ref[:, j, :]


def to_field(rows_ref, field_ref):
    for j in range(JL):
        field_ref[:, j, :] = rows_ref[j * CL : (j + 1) * CL, :]


def middle(grid_ref, x_ref, cot_ref, f_ref, y_ref, slope_ref):
    for first, width in CHUNKS:
        cols = slice(first, first + width)
        v = dot(grid_ref[...], f_ref[:, cols])
        cdf = 0.5 * (1.0 + lax.erf(v * (1.0 / math.sqrt(2.0))))
        y_ref[:, cols] = (x_ref[:, cols].astype(F32) + v * cdf).astype(BF)
        slope = cdf + v * jnp.exp(-0.5 * v * v) * (1.0 / math.sqrt(2.0 * math.pi))
        slope_ref[:, cols] = (cot_ref[:, cols].astype(F32) * slope).astype(BF)


def last(grid_ref, cot_ref, f_ref, out_ref):
    for first, width in CHUNKS:
        cols = slice(first, first + width)
        v = dot(grid_ref[...], f_ref[:, cols])
        out_ref[:, cols] = (cot_ref[:, cols].astype(F32) + v).astype(BF)


def mixing_weights(weights, w2_ref):
    zero = jnp.zeros((CL, CL), F32)
    for x in range(NX):
        slab = weights[x * CL : (x + 1) * CL, :]
        pieces = [slab[:, i * CL : (i + 1) * CL] for i in range(NX)]
        top = jnp.concatenate([a for p in pieces for a in (p, zero)], axis=1)
        low = jnp.concatenate([a for p in pieces for a in (zero, p)], axis=1)
        w2_ref[x * 128 : x * 128 + CL, :] = top.astype(BF)
        w2_ref[x * 128 + CL : (x + 1) * 128, :] = low.astype(BF)


def split_gain(gain_ref, out_ref):
    turned = jnp.transpose(gain_ref[...])
    high = turned.astype(BF).astype(F32)
    out_ref[...] = jnp.concatenate([high, turned - high], axis=1).astype(BF)


def gain_rows(shift_ref, garr_ref, rows_ref):
    both = dot(shift_ref[...], flat(garr_ref))
    for x in range(NX):
        row = both[:, x * 128 : x * 128 + CL] + both[:, x * 128 + CL : (x + 1) * 128]
        rows_ref[:, x * 128 : (x + 1) * 128] = jnp.concatenate([row, row], axis=1)


def gain_sums(grad_ref, mixed_ref, shift_t_ref, sums_ref):
    parts = []
    for x in range(NX):
        cols = slice(x * 128, (x + 1) * 128)
        prod = grad_ref[:, cols] * mixed_ref[:, cols].astype(F32)
        prod = prod[:, :CL] + prod[:, CL:]
        high = prod.astype(BF).astype(F32)
        parts.append(jnp.concatenate([high, prod - high], axis=1).astype(BF))
    both = dot(shift_t_ref[...], jnp.concatenate(parts, axis=1))
    for x in range(NX):
        row = both[:, x * 128 : x * 128 + CL] + both[:, x * 128 + CL : (x + 1) * 128]
        sums_ref[x, 128:384, :] = jnp.concatenate([row[:256], row[256:]], axis=1).astype(BF)


def mix_sums(coeff_t_ref, pre_ref, sums_ref):
    mix = dot(coeff_t_ref[...], pre_ref[...])
    for x in range(NX):
        blocks = []
        for i in range(NX):
            a = mix[i * 128 : i * 128 + CL, x * 128 : x * 128 + CL]
            b = mix[i * 128 + CL : (i + 1) * 128, x * 128 + CL : (x + 1) * 128]
            blocks.append(a + b)
        low = jnp.concatenate([blocks[0], blocks[1]], axis=0)
        high = jnp.concatenate([blocks[2], blocks[3]], axis=0)
        sums_ref[x, 0:128, :] = jnp.concatenate([low, high], axis=1).astype(BF)


def flat(q_ref):
    return jnp.concatenate([q_ref[x] for x in range(NX)], axis=1)


def split_lanes(value, scale, ref):
    for x in range(NX):
        part = value[:, x * 128 : (x + 1) * 128]
        ref[x] = (part if scale is None else part * scale).astype(BF)


class Place:
    def __init__(self):
        lat = lax.axis_index("lat")
        self.x = lax.axis_index("ch")
        self.c = lax.rem(lat, 2)
        self.y = lax.rem(lax.div(lat, 2), 8)
        self.z = lax.div(lat, 16)
        self.major = jnp.where(self.c == 0, self.z, self.y)

    def at(self, z=None, y=None, c=None, x=None):
        z, y = (self.z if z is None else z), (self.y if y is None else y)
        c, x = (self.c if c is None else c), (self.x if x is None else x)
        return ((z * 8 + y) * 2 + c, x)


NEAR = (0, 1, 7, 2, 6, 3, 5, 4)
FAR = (4, 3, 5, 2, 6, 1, 7, 0)


def around(value, step, count):
    return lax.rem(value + step, count)


def send(src, dst, ssem, rsem, target):
    pltpu.make_async_remote_copy(
        src_ref=src, dst_ref=dst, send_sem=ssem, recv_sem=rsem, device_id=target, device_id_type=MESH
    ).start()


def settle(view, sem):
    pltpu.make_async_copy(view, view, sem).wait()


def greet(me):
    barrier = pltpu.get_barrier_semaphore()
    other = 1 - me.c
    targets = [me.at(c=other)]
    for o in range(1, 8):
        targets += [me.at(y=around(me.y, o, 8)), me.at(z=around(me.z, o, 8))]
        targets += [me.at(y=around(me.y, o, 8), c=other), me.at(z=around(me.z, o, 8), c=other)]
    for o in range(1, 4):
        targets.append(me.at(x=around(me.x, o, 4)))
    for target in targets:
        pl.semaphore_signal(barrier, inc=1, device_id=target, device_id_type=MESH)
    return len(targets)


def orders_first(me, s_ref, ta_ref, tb_ref, ssem, rsem, lsem):
    pltpu.make_async_copy(s_ref.at[:, me.y, 0], ta_ref.at[me.y], lsem.at[0]).start()
    pltpu.make_async_copy(s_ref.at[me.z, :, 1], tb_ref.at[me.z], lsem.at[1]).start()
    for o in FAR[:7]:
        y, z = around(me.y, o, 8), around(me.z, o, 8)
        send(s_ref.at[:, y, 0], ta_ref.at[me.y], ssem.at[0], rsem.at[0], me.at(y=y))
        send(s_ref.at[z, :, 1], tb_ref.at[me.z], ssem.at[1], rsem.at[1], me.at(z=z))


def orders_second(me, ta_ref, tb_ref, r_ref, ssem, gsem, rsem, lsem):
    settle(ta_ref.at[0], lsem.at[0])
    settle(ta_ref.at[0:7], rsem.at[0])
    settle(tb_ref.at[0], lsem.at[1])
    settle(tb_ref.at[0:7], rsem.at[1])
    here_a, here_b = r_ref.at[me.z, :, me.c], r_ref.at[me.y, :, me.c]
    to_a, to_b = 2 + me.c, 3 - me.c

    @pl.when(me.c == 0)
    def _():
        pltpu.make_async_copy(ta_ref.at[:, me.z], here_a, lsem.at[2]).start()
        send(tb_ref.at[:, me.y], here_b, ssem.at[3], gsem.at[me.y], me.at(c=1))

    @pl.when(me.c == 1)
    def _():
        pltpu.make_async_copy(tb_ref.at[:, me.y], here_b, lsem.at[2]).start()
        send(ta_ref.at[:, me.z], here_a, ssem.at[3], gsem.at[me.z], me.at(c=0))

    for o in NEAR[1:]:
        y, z = around(me.y, o, 8), around(me.z, o, 8)
        send(ta_ref.at[:, z], here_a, ssem.at[to_a], gsem.at[me.z], me.at(z=z, c=0))
        send(tb_ref.at[:, y], here_b, ssem.at[to_b], gsem.at[me.y], me.at(y=y, c=1))


def orders_third(me, r_ref, perm_ref, p_ref, q_ref, gsem, lsem, xs, xr):
    for o in NEAR:
        g = around(me.major, o, 8)
        if o == 0:
            settle(r_ref.at[0, :, 0], lsem.at[2])
            settle(r_ref.at[0, :, 0], gsem.at[g])
        else:
            settle(r_ref.at[0], gsem.at[g])
        out = dot(perm_ref[...], r_ref[g].reshape(256, 128)).astype(BF)
        at = pl.ds(pl.multiple_of(g * 64, 64), 64)
        for s in range(4):
            p_ref[s, at, :] = out[s * 64 : (s + 1) * 64]
        for k in (2, 1, 3):
            x = around(me.x, k, 4)
            send(p_ref.at[x, at], q_ref.at[me.x, at], xs, xr, me.at(x=x))
        q_ref[me.x, at, :] = p_ref[me.x, at, :]


def lat_sent(ta_ref, ssem):
    settle(ta_ref.at[0:7], ssem.at[0])
    settle(ta_ref.at[0:7], ssem.at[1])
    settle(ta_ref.at[0:7], ssem.at[2])
    settle(ta_ref, ssem.at[3])


def grid_first(me, ret_ref, p_ref, xs, gsem):
    for o in FAR:
        g = around(me.major, o, 8)
        at = pl.ds(pl.multiple_of(g * 64, 64), 64)
        for k in (2, 1, 3):
            x = around(me.x, k, 4)
            send(ret_ref.at[x, at], p_ref.at[me.x, at], xs, gsem.at[g], me.at(x=x))
    p_ref[me.x] = ret_ref[me.x]


def grid_second(me, p_ref, perm_ref, s_ref, t_ref, ssem, rsem, gsem, lsem):
    here = t_ref.at[me.c, me.major]
    for o in FAR:
        g = around(me.major, o, 8)
        at = pl.ds(pl.multiple_of(g * 64, 64), 64)
        settle(p_ref.at[0:3, 0:64], gsem.at[g])
        rows = jnp.concatenate([p_ref[s, at, :] for s in range(4)], axis=0)
        s_ref[g] = dot(perm_ref[...], rows, TN).astype(BF).reshape(8, 2, 16, 128)
        z, y = jnp.where(me.c == 0, g, me.z), jnp.where(me.c == 0, me.y, g)
        other = 1 - me.c
        send(s_ref.at[g, :, other], here, ssem.at[3], rsem.at[3], me.at(z=z, y=y, c=other))
        if o == 0:
            pltpu.make_async_copy(s_ref.at[g, :, me.c], here, lsem.at[0]).start()
        else:
            send(s_ref.at[g, :, me.c], here, ssem.at[2], rsem.at[2], me.at(z=z, y=y))


def grid_third(me, t_ref, r_ref, ssem, rsem, lsem):
    settle(t_ref.at[0, 0], lsem.at[0])
    settle(t_ref.at[0, 0:7], rsem.at[2])
    settle(t_ref.at[0], rsem.at[3])
    here_a, here_b = r_ref.at[:, me.y, 0], r_ref.at[me.z, :, 1]
    for o in FAR[:7]:
        y, z = around(me.y, o, 8), around(me.z, o, 8)
        send(t_ref.at[0, :, y], here_a, ssem.at[0], rsem.at[0], me.at(y=y))
        send(t_ref.at[1, :, z], here_b, ssem.at[1], rsem.at[1], me.at(z=z))
    pltpu.make_async_copy(t_ref.at[0, :, me.y], here_a, lsem.at[1]).start()
    pltpu.make_async_copy(t_ref.at[1, :, me.z], here_b, lsem.at[2]).start()


def grid_end(t_ref, rsem, lsem):
    settle(t_ref.at[0, 0], lsem.at[1])
    settle(t_ref.at[0, 0], lsem.at[2])
    settle(t_ref.at[0, 0:7], rsem.at[0])
    settle(t_ref.at[0, 0:7], rsem.at[1])


def x_start(me, src_ref, dst_ref, ssem, rsem, lsem):
    for o in (2, 1, 3):
        x = around(me.x, o, 4)
        send(src_ref.at[x], dst_ref.at[me.x], ssem, rsem, me.at(x=x))
    pltpu.make_async_copy(src_ref.at[me.x], dst_ref.at[me.x], lsem).start()


def x_end(dst_ref, rsem, lsem):
    settle(dst_ref.at[0], lsem)
    settle(dst_ref.at[0:3], rsem)


def whole_kernel(
    slots_ref, logs_ref, mrow_ref, cosv_ref, logsin_ref, band_ref, sine_ref, perm_ref, turn_ref, w_ref, gain_ref, xfield_ref, cfield_ref,
    yfield_ref, spectrum_ref, out_ref, mix_ref, ggain_ref,
    x_ref, cot_ref, y_ref,
    f_ref, mcol_ref, up_ref, low_ref, raw_ref, l_ref, lt_ref, shift_ref, shift_t_ref, w2_ref, w2t_ref, gsend_ref, garr_ref, grows_ref,
    stage_ref, grid_ref, slope_ref, coeff_ref, coeff_t_ref, mixed_ref, flat_ref, pre_ref, grad_ref, spec_ref, ret_ref, ret2_ref,
    s_refs, ta_refs, tb_refs, t_refs, r_refs, p_refs, q_refs,
    sums_ref, v_ref, own_ref, ybuf_ref, piece_ref, zbuf_ref, fin_ref, total_ref,
    ssem, rsem, gsem, lsem, xs, xr, xl, gs, gr,
):
    me = Place()
    other = 1 - me.c
    peers = greet(me)
    lat = lax.axis_index("lat")
    order = slots_ref[lat * NX + me.x]
    m = order.astype(F32)
    mrow = mrow_ref[...]
    half_row = jnp.where(mrow == 0, 0.5, 1.0)
    mcol_ref[...] = jnp.transpose(jnp.broadcast_to(mrow.astype(F32), (128, MODES)))
    split_gain(gain_ref, gsend_ref)
    long_tables(mcol_ref, f_ref)

    sines = band_ref[pl.ds(lat, 1), :]
    to_rows(xfield_ref, x_ref)
    g = dot(f_ref[...], x_ref[...], NT) * sines
    pack_blocks(g, perm_ref, s_refs.at[0], stage_ref)
    pl.semaphore_wait(pltpu.get_barrier_semaphore(), peers)

    def xlinks(i):
        return xs.at[i], xr.at[i], xl.at[i]

    def begin(i):
        orders_first(me, s_refs.at[i], ta_refs.at[i // 2], tb_refs.at[i // 2], ssem.at[i], rsem.at[i], lsem.at[i])

    def carry_on(i):
        refs = ta_refs.at[i // 2], tb_refs.at[i // 2], r_refs.at[i]
        orders_second(me, *refs, ssem.at[i], gsem.at[i], rsem.at[i], lsem.at[i])
        refs = r_refs.at[i], turn_ref, p_refs.at[i], q_refs.at[i // 2]
        orders_third(me, *refs, gsem.at[i], lsem.at[i], xs.at[i], xr.at[i])

    def back_on(i):
        refs = p_refs.at[i], turn_ref, s_refs.at[i], t_refs.at[i // 2]
        grid_second(me, *refs, ssem.at[i], rsem.at[i], gsem.at[i], lsem.at[i])

    def back_out(i):
        grid_third(me, t_refs.at[i // 2], r_refs.at[i], ssem.at[i], rsem.at[i], lsem.at[i])

    def back_end(i):
        grid_end(t_refs.at[i // 2], rsem.at[i], lsem.at[i])

    begin(0)
    for o in range(1, 4):
        x = around(me.x, o, 4)
        send(gsend_ref, garr_ref.at[me.x], xs.at[6], xr.at[6], me.at(x=x))
    garr_ref[me.x] = gsend_ref[...]
    to_rows(cfield_ref, cot_ref)
    weights = w_ref[...].astype(F32)
    mixing_weights(weights, w2_ref)
    mixing_weights(jnp.transpose(weights), w2t_ref)
    carry = legendre_start(m, logs_ref[order], logsin_ref[me.c], up_ref, low_ref)
    legendre_steps(0, MODES // RENEW, carry, cosv_ref[me.c], up_ref, low_ref, raw_ref)
    legendre_end(order, raw_ref, l_ref, lt_ref, shift_ref, shift_t_ref)
    carry_on(0)
    settle(garr_ref.at[0:3], xr.at[6])
    gain_rows(shift_ref, garr_ref, grows_ref)
    settle(q_refs.at[0, 0:3], xr.at[0])

    coeff_ref[...] = dot(l_ref[...], flat(q_refs.at[0])).astype(BF)
    mixed_ref[...] = dot(coeff_ref[...], w2_ref[...]).astype(BF)
    flat_ref[...] = (mixed_ref[...].astype(F32) * grows_ref[...]).astype(BF)
    split_lanes(dot(lt_ref[...], flat_ref[...]), None, ret_ref)
    grid_first(me, ret_ref, p_refs.at[1], xs.at[1], gsem.at[1])
    back_on(1)
    back_out(1)
    for x in range(NX):
        cols = slice(x * 128, (x + 1) * 128)
        spec_ref[x] = jnp.transpose(flat_ref[:, cols].astype(F32)).astype(BF)
        coeff_t_ref[cols, :] = jnp.transpose(coeff_ref[:, cols].astype(F32)).astype(BF)
    x_start(me, spec_ref, spectrum_ref, *xlinks(4))
    back_end(1)

    unpack_blocks(r_refs.at[1], perm_ref, half_row, grid_ref)
    middle(grid_ref, x_ref, cot_ref, f_ref, y_ref, slope_ref)
    mcol = mcol_ref[...]
    half_col = jnp.where(jnp.concatenate([mcol, mcol], axis=1) == 0.0, 0.5, 1.0)
    half_col = jnp.concatenate([half_col, half_col], axis=0)
    g = dot(f_ref[...], slope_ref[...], NT) * half_col
    pack_blocks(g, perm_ref, s_refs.at[2], stage_ref)
    begin(2)
    to_field(y_ref, yfield_ref)
    carry_on(2)
    settle(q_refs.at[1, 0:3], xr.at[2])

    grad_ref[...] = dot(l_ref[...], flat(q_refs.at[1]))
    pre_ref[...] = (grad_ref[...] * grows_ref[...]).astype(BF)
    back = dot(pre_ref[...], w2t_ref[...]).astype(BF)
    split_lanes(dot(lt_ref[...], back), sine_ref[me.c], ret2_ref)
    grid_first(me, ret2_ref, p_refs.at[3], xs.at[3], gsem.at[3])
    gain_sums(grad_ref, mixed_ref, shift_t_ref, sums_ref)
    mix_sums(coeff_t_ref, pre_ref, sums_ref)
    x_start(me, sums_ref, v_ref, *xlinks(5))
    back_on(3)
    back_out(3)
    x_end(v_ref, xr.at[5], xl.at[5])
    own_ref[...] = sum(v_ref[x].astype(F32) for x in range(NX)).reshape(2, 8, 24, 128)
    for o in FAR:
        y = around(me.y, o, 8)
        if o > 0:
            send(own_ref.at[me.c, y], ybuf_ref.at[me.c, me.y], gs.at[0], gr.at[0], me.at(y=y))
        send(own_ref.at[other, y], ybuf_ref.at[me.c, me.y], gs.at[1], gr.at[1], me.at(y=y, c=other))
    ybuf_ref[me.c, me.y] = own_ref[me.c, me.y]
    settle(ybuf_ref.at[0, 0:7], gr.at[0])
    settle(ybuf_ref.at[0], gr.at[1])
    piece_ref[...] = jnp.sum(ybuf_ref[0] + ybuf_ref[1], axis=0)
    for o in range(1, 8):
        z = around(me.z, o, 8)
        send(piece_ref, zbuf_ref.at[me.z], gs.at[2], gr.at[2], me.at(z=z))
    zbuf_ref[me.z] = piece_ref[...]
    settle(zbuf_ref.at[0:7], gr.at[2])
    fin_ref[...] = jnp.sum(zbuf_ref[...], axis=0)
    for o in range(8):
        y = around(me.y, o, 8)
        if o > 0:
            send(fin_ref, total_ref.at[me.c, me.y], gs.at[3], gr.at[3], me.at(y=y))
        send(fin_ref, total_ref.at[me.c, me.y], gs.at[4], gr.at[4], me.at(y=y, c=other))
    total_ref[me.c, me.y] = fin_ref[...]
    back_end(3)

    unpack_blocks(r_refs.at[3], perm_ref, None, grid_ref)
    last(grid_ref, cot_ref, f_ref, out_ref)
    settle(total_ref.at[0, 0:7], gr.at[3])
    settle(total_ref.at[0], gr.at[4])
    mix = total_ref[0].reshape(192, 128)[0:128] * (1.0 / MODES)
    mix_ref[...] = jnp.transpose(jnp.concatenate([mix[:, :CL], mix[:, CL:]], axis=0))
    gain = jnp.concatenate([total_ref[0].reshape(192, 128)[128:192], total_ref[1].reshape(192, 128)], axis=0)
    gain = jnp.concatenate([gain[:, :CL], gain[:, CL:]], axis=0) * (1.0 / math.sqrt(MODES))
    ggain_ref[...] = jnp.transpose(gain)

    for i in range(4):
        lat_sent(ta_refs.at[0], ssem.at[i])
    x_end(spectrum_ref, xr.at[4], xl.at[4])
    for i in range(5):
        settle(p_refs.at[0, 0:3], xs.at[i])
    settle(v_ref.at[0:3], xs.at[5])
    settle(garr_ref.at[0:3], xs.at[6])
    settle(ybuf_ref.at[0, 0:7], gs.at[0])
    settle(ybuf_ref.at[0], gs.at[1])
    settle(zbuf_ref.at[0:7], gs.at[2])
    settle(total_ref.at[0, 0:7], gs.at[3])
    settle(total_ref.at[0], gs.at[4])


VM = pl.BlockSpec(memory_space=pltpu.VMEM)
SM = pl.BlockSpec(memory_space=pltpu.SMEM)


def whole(*operands):
    scratch = [
        *[((256, NLON), BF)] * 3,
        ((2 * MODES, NLON), BF), ((MODES, 128), F32), ((MODES, 128), F32), ((MODES, 128), F32), ((MODES * 4, 128), F32),
        *[((512, 512), BF)] * 6, ((512, 128), BF), ((4, 512, 128), BF),
        ((512, 512), F32),
        ((4, 512, 128), BF), ((256, 1024), BF), ((256, NLON), BF), ((512, 512), BF), ((512, 512), BF), ((512, 512), BF), ((512, 512), BF),
        ((512, 512), BF), ((512, 512), F32), ((4, 128, 512), BF), ((4, 512, 128), BF), ((4, 512, 128), BF),
        ((4, NZ, NY, NC, 16, 128), BF), ((2, 8, 8, 16, 128), BF), ((2, 8, 8, 16, 128), BF), ((2, 2, 8, 8, 16, 128), BF),
        ((4, NZ, NY, NC, 16, 128), BF),
        ((4, 4, 512, 128), BF), ((2, 4, 512, 128), BF),
        ((4, 384, 128), BF), ((4, 384, 128), BF), ((2, 8, 24, 128), F32), ((2, 8, 24, 128), F32),
        ((24, 128), F32), ((8, 24, 128), F32), ((24, 128), F32), ((2, 8, 24, 128), F32),
    ]
    sems = [(4, 4), (4, 4), (4, 8), (4, 3), (7,), (7,), (7,), (5,), (5,)]
    outs = [((CL, JL, NLON), BF), ((4, 128, 512), BF), ((256, NLON), BF), ((64, 256), F32), ((64, 512), F32)]
    return pl.pallas_call(
        whole_kernel,
        out_shape=tuple(jax.ShapeDtypeStruct(*o) for o in outs),
        in_specs=[SM, SM] + [VM] * (len(operands) - 2),
        out_specs=tuple(VM for _ in outs),
        scratch_shapes=[pltpu.VMEM(*s) for s in scratch] + [pltpu.SemaphoreType.DMA(s) for s in sems],
        compiler_params=pltpu.CompilerParams(vmem_limit_bytes=VMEM_BYTES, collective_id=0, has_side_effects=True),
        name="whole",
    )(*operands)


def finish_kernel(y_in, spec_in, grad_in, mix_in, gain_in, y_out, spec_out, grad_out, mix_out, gain_out):
    y_out[...] = y_in[...]
    spec_out[...] = spec_in[...]
    to_field(grad_in, grad_out)
    mix_out[...] = mix_in[...]
    gain_out[...] = gain_in[...]


def finish(y, spectrum, grad, mix, gain):
    outs = [((CL, JL, NLON), BF), ((4, 128, 512), BF), ((CL, JL, NLON), BF), ((64, 256), F32), ((64, 512), F32)]
    return pl.pallas_call(
        finish_kernel,
        out_shape=tuple(jax.ShapeDtypeStruct(*o) for o in outs),
        in_specs=[VM] * 5,
        out_specs=(VM,) * 5,
        compiler_params=pltpu.CompilerParams(vmem_limit_bytes=VMEM_BYTES),
        name="finish",
    )(y, spectrum, grad, mix, gain)


def one_hot(rows):
    out = np.zeros((rows.size, rows.size), np.float32)
    out[np.arange(rows.size), rows] = 1.0
    return jnp.asarray(out, BF)


def body(grid_field, order_slots, mix_weight, degree_gain, cotangent):
    d, s, j = np.meshgrid(np.arange(32), np.arange(4), np.arange(4), indexing="ij")
    perm = one_hot((j * 128 + d * 4 + s).reshape(-1))
    s, e, j = np.meshgrid(np.arange(4), np.arange(16), np.arange(4), indexing="ij")
    turn = one_hot((e * 16 + s * 4 + j).reshape(-1))
    theta = math.pi * (np.arange(NLAT) + 0.5) / NLAT
    both = np.stack([theta, theta.reshape(8, 8, 8).transpose(1, 0, 2).reshape(-1)])
    cosv = jnp.asarray(np.cos(both).reshape(2, 4, 128), F32)
    logsin = jnp.asarray(np.log(np.sin(both)).reshape(2, 4, 128), F32)
    band = jnp.asarray(np.repeat(np.sin(theta).reshape(128, JL), CL, axis=1), F32)
    sine_col = jnp.asarray(np.repeat(np.sin(both).reshape(2, NLAT, 1), 128, axis=2), F32)
    n = np.arange(1, MODES)
    logs = jnp.asarray(np.concatenate([[0.0], np.cumsum(np.log((2.0 * n - 1.0) / (2.0 * n)))]), F32)
    out, spectrum, grad, mix, gain = whole(
        order_slots, logs, order_slots.reshape(1, MODES), cosv, logsin, band, sine_col, perm, turn,
        mix_weight, degree_gain, grid_field, cotangent,
    )
    out, spectrum, grad, mix, gain = finish(out, spectrum, grad, mix, gain)
    return out, spectrum.reshape(4, 2, CL, MODES), grad, mix.T, gain


def solution(mesh):
    placed = (P("ch", "lat", None), P(), P(), P("ch", None), P("ch", "lat", None))
    return jax.shard_map(
        body,
        mesh=mesh,
        in_specs=placed,
        out_specs=(
            P("ch", "lat", None),
            P("lat", None, "ch", None),
            P("ch", "lat", None),
            P(None, "ch"),
            P("ch", None),
        ),
        check_vma=False,
    )
```

```python
import math

import jax
import jax.numpy as jnp
import numpy as np
from jax import lax
from jax.experimental import pallas as pl
from jax.experimental.pallas import tpu as pltpu
from jax.sharding import PartitionSpec as P

MESH = pl.DeviceIdType.MESH
BF, F32 = jnp.bfloat16, jnp.float32
CL, JL, NLON = 64, 4, 1440
NZ, NY, NC, NX = 8, 8, 2, 4
NLAT, MODES = 512, 512
RENEW = 32
VMEM_BYTES = 56 * 1024 * 1024
NN = (((1,), (0,)), ((), ()))
NT = (((1,), (1,)), ((), ()))
TN = (((0,), (0,)), ((), ()))


def dot(a, b, dims=NN):
    return lax.dot_general(a, b, dims, preferred_element_type=F32)


def half_angle(steps):
    turns = jnp.floor(steps * (1.0 / NLON) + 0.5)
    t = (steps - turns * NLON) * (math.pi / NLON)
    u = t * t
    s = t * (1.0 + u * (-1.0 / 6 + u * (1.0 / 120 + u * (-1.0 / 5040 + u * (1.0 / 362880 + u * (-1.0 / 39916800))))))
    c = 1.0 + u * (-0.5 + u * (1.0 / 24 + u * (-1.0 / 720 + u * (1.0 / 40320 + u * (-1.0 / 3628800 + u * (1.0 / 479001600))))))
    return 1.0 - 2.0 * s * s, 2.0 * s * c


def long_tables(mcol_ref, f_ref):
    def long_rows(i, carry):
        rows = pl.ds(pl.multiple_of(i * 64, 64), 64)
        lower = pl.ds(pl.multiple_of(i * 64 + MODES, 64), 64)
        mc = mcol_ref[rows, :]
        lane = lax.broadcasted_iota(jnp.int32, (64, 128), 1).astype(F32)
        cb, sb = half_angle(mc * lane)
        ca, sa = half_angle(mc * (lane * 128.0))
        cb, sb = cb * math.sqrt(2.0 / NLON), sb * math.sqrt(2.0 / NLON)
        for a in range(12):
            width = min(128, NLON - a * 128)
            cav = jnp.broadcast_to(ca[:, a : a + 1], (64, 128))
            sav = jnp.broadcast_to(sa[:, a : a + 1], (64, 128))
            f_ref[rows, a * 128 : a * 128 + width] = (cav * cb - sav * sb).astype(BF)[:, :width]
            f_ref[lower, a * 128 : a * 128 + width] = (-(sav * cb + cav * sb)).astype(BF)[:, :width]
        return carry

    lax.fori_loop(0, 8, long_rows, 0)


def legendre_start(m, logs, logsin, up_ref, low_ref):
    k = lax.broadcasted_iota(jnp.int32, (MODES, 128), 0).astype(F32)
    degree = k + (m + 1.0)
    upper = jnp.sqrt((4.0 * degree * degree - 1.0) / (degree * degree - m * m))
    below = degree - 1.0
    lower = jnp.sqrt((below * below - m * m) / jnp.maximum(4.0 * below * below - 1.0, 1.0))
    up_ref[...] = upper
    low_ref[...] = upper * lower
    start = 0.5 * (jnp.log(jnp.full((4, 128), m + 0.5, F32)) + logs) + m * logsin
    zero = jnp.zeros((4, 128), F32)
    return zero, zero + 1.0, start


def legendre_steps(first, last, carry, cosv, up_ref, low_ref, raw_ref):
    def block(b, carry):
        previous, current, scale = carry
        factor = jnp.exp(0.5 * scale)
        for offset in range(RENEW):
            step = b * RENEW + offset
            raw_ref[pl.ds(pl.multiple_of(step * 4, 4), 4), :] = current * factor * factor
            ua = jnp.broadcast_to(up_ref[pl.ds(step, 1), :], (4, 128)) * cosv
            lb = jnp.broadcast_to(low_ref[pl.ds(step, 1), :], (4, 128))
            previous, current = current, ua * current - lb * previous
        biggest = jnp.maximum(jnp.abs(previous), jnp.abs(current))
        shift = jnp.log(biggest)
        rescale = jnp.exp(-shift)
        return previous * rescale, current * rescale, scale + shift

    return lax.fori_loop(first, last, block, carry)


def legendre_end(order, raw_ref, l_ref, lt_ref, shift_ref, shift_t_ref):
    live = lax.broadcasted_iota(jnp.int32, (MODES, 128), 0) < MODES - order
    for g in range(4):
        part = raw_ref[pl.ds(g, MODES, stride=4), :]
        part = jnp.where(live, part, 0.0) * math.sqrt(math.pi / NLAT)
        l_ref[:, g * 128 : (g + 1) * 128] = part.astype(BF)
        lt_ref[g * 128 : (g + 1) * 128, :] = jnp.transpose(part).astype(BF)
    k = lax.broadcasted_iota(jnp.int32, (MODES, MODES), 0)
    l = lax.broadcasted_iota(jnp.int32, (MODES, MODES), 1)
    shift_ref[...] = jnp.where(l - k == order, 1.0, 0.0).astype(BF)
    shift_t_ref[...] = jnp.where(k - l == order, 1.0, 0.0).astype(BF)


def pack_blocks(g, perm_ref, s_ref, stage_ref):
    for j in range(JL):
        cols = slice(j * CL, (j + 1) * CL)
        stage_ref[j] = jnp.concatenate([g[:MODES, cols], g[MODES:, cols]], axis=1).astype(BF)
    for g in range(4):
        rows = jnp.concatenate([stage_ref[j, g * 128 : (g + 1) * 128, :] for j in range(JL)], axis=0)
        s_ref[2 * g : 2 * g + 2] = dot(perm_ref[...], rows).astype(BF).reshape(2, 8, 2, 16, 128)


def unpack_blocks(r_ref, perm_ref, half, grid_ref):
    for g in range(4):
        rows = r_ref[2 * g : 2 * g + 2].reshape(512, 128)
        turned = dot(rows, perm_ref[...], TN)
        for j in range(JL):
            piece = turned[:, j * 128 : (j + 1) * 128]
            if half is not None:
                piece = piece * half[:, g * 128 : (g + 1) * 128]
            piece = piece.astype(BF)
            for r in range(2):
                at = r * MODES + g * 128
                grid_ref[j * CL : (j + 1) * CL, at : at + 128] = piece[r * CL : (r + 1) * CL]


CHUNKS = ((0, 384), (384, 384), (768, 384), (1152, 288))


def to_rows(field_ref, rows_ref):
    for j in range(JL):
        rows_ref[j * CL : (j + 1) * CL, :] = field_ref[:, j, :]


def to_field(rows_ref, field_ref):
    for j in range(JL):
        field_ref[:, j, :] = rows_ref[j * CL : (j + 1) * CL, :]


def middle(grid_ref, x_ref, cot_ref, f_ref, y_ref, slope_ref):
    for first, width in CHUNKS:
        cols = slice(first, first + width)
        v = dot(grid_ref[...], f_ref[:, cols])
        cdf = 0.5 * (1.0 + lax.erf(v * (1.0 / math.sqrt(2.0))))
        y_ref[:, cols] = (x_ref[:, cols].astype(F32) + v * cdf).astype(BF)
        slope = cdf + v * jnp.exp(-0.5 * v * v) * (1.0 / math.sqrt(2.0 * math.pi))
        slope_ref[:, cols] = (cot_ref[:, cols].astype(F32) * slope).astype(BF)


def last(grid_ref, cot_ref, f_ref, out_ref):
    for first, width in CHUNKS:
        cols = slice(first, first + width)
        v = dot(grid_ref[...], f_ref[:, cols])
        out_ref[:, cols] = (cot_ref[:, cols].astype(F32) + v).astype(BF)


def mixing_weights(weights, w2_ref):
    zero = jnp.zeros((CL, CL), F32)
    for x in range(NX):
        slab = weights[x * CL : (x + 1) * CL, :]
        pieces = [slab[:, i * CL : (i + 1) * CL] for i in range(NX)]
        top = jnp.concatenate([a for p in pieces for a in (p, zero)], axis=1)
        low = jnp.concatenate([a for p in pieces for a in (zero, p)], axis=1)
        w2_ref[x * 128 : x * 128 + CL, :] = top.astype(BF)
        w2_ref[x * 128 + CL : (x + 1) * 128, :] = low.astype(BF)


def split_gain(gain_ref, out_ref):
    turned = jnp.transpose(gain_ref[...])
    high = turned.astype(BF).astype(F32)
    out_ref[...] = jnp.concatenate([high, turned - high], axis=1).astype(BF)


def gain_rows(shift_ref, garr_ref, rows_ref):
    both = dot(shift_ref[...], flat(garr_ref))
    for x in range(NX):
        row = both[:, x * 128 : x * 128 + CL] + both[:, x * 128 + CL : (x + 1) * 128]
        rows_ref[:, x * 128 : (x + 1) * 128] = jnp.concatenate([row, row], axis=1)


def gain_sums(grad_ref, mixed_ref, shift_t_ref, sums_ref):
    parts = []
    for x in range(NX):
        cols = slice(x * 128, (x + 1) * 128)
        prod = grad_ref[:, cols] * mixed_ref[:, cols].astype(F32)
        prod = prod[:, :CL] + prod[:, CL:]
        high = prod.astype(BF).astype(F32)
        parts.append(jnp.concatenate([high, prod - high], axis=1).astype(BF))
    both = dot(shift_t_ref[...], jnp.concatenate(parts, axis=1))
    for x in range(NX):
        row = both[:, x * 128 : x * 128 + CL] + both[:, x * 128 + CL : (x + 1) * 128]
        sums_ref[x, 128:384, :] = jnp.concatenate([row[:256], row[256:]], axis=1).astype(BF)


def mix_sums(coeff_t_ref, pre_ref, sums_ref):
    mix = dot(coeff_t_ref[...], pre_ref[...])
    for x in range(NX):
        blocks = []
        for i in range(NX):
            a = mix[i * 128 : i * 128 + CL, x * 128 : x * 128 + CL]
            b = mix[i * 128 + CL : (i + 1) * 128, x * 128 + CL : (x + 1) * 128]
            blocks.append(a + b)
        low = jnp.concatenate([blocks[0], blocks[1]], axis=0)
        high = jnp.concatenate([blocks[2], blocks[3]], axis=0)
        sums_ref[x, 0:128, :] = jnp.concatenate([low, high], axis=1).astype(BF)


def flat(q_ref):
    return jnp.concatenate([q_ref[x] for x in range(NX)], axis=1)


def split_lanes(value, scale, ref):
    for x in range(NX):
        part = value[:, x * 128 : (x + 1) * 128]
        ref[x] = (part if scale is None else part * scale).astype(BF)


class Place:
    def __init__(self):
        lat = lax.axis_index("lat")
        self.x = lax.axis_index("ch")
        self.c = lax.rem(lat, 2)
        self.y = lax.rem(lax.div(lat, 2), 8)
        self.z = lax.div(lat, 16)
        self.major = jnp.where(self.c == 0, self.z, self.y)

    def at(self, z=None, y=None, c=None, x=None):
        z, y = (self.z if z is None else z), (self.y if y is None else y)
        c, x = (self.c if c is None else c), (self.x if x is None else x)
        return ((z * 8 + y) * 2 + c, x)


NEAR = (0, 1, 7, 2, 6, 3, 5, 4)
FAR = (4, 3, 5, 2, 6, 1, 7, 0)


def around(value, step, count):
    return lax.rem(value + step, count)


def send(src, dst, ssem, rsem, target):
    pltpu.make_async_remote_copy(
        src_ref=src, dst_ref=dst, send_sem=ssem, recv_sem=rsem, device_id=target, device_id_type=MESH
    ).start()


def settle(view, sem):
    pltpu.make_async_copy(view, view, sem).wait()


def greet(me):
    barrier = pltpu.get_barrier_semaphore()
    other = 1 - me.c
    targets = [me.at(c=other)]
    for o in range(1, 8):
        targets += [me.at(y=around(me.y, o, 8)), me.at(z=around(me.z, o, 8))]
        targets += [me.at(y=around(me.y, o, 8), c=other), me.at(z=around(me.z, o, 8), c=other)]
    for o in range(1, 4):
        targets.append(me.at(x=around(me.x, o, 4)))
    for target in targets:
        pl.semaphore_signal(barrier, inc=1, device_id=target, device_id_type=MESH)
    return len(targets)


def orders_first(me, s_ref, ta_ref, tb_ref, ssem, rsem, lsem):
    view = s_ref.reshape(4, 2, 4, 2, NC, 16, 128)

    def row(p, y):
        return view.at[:, p, lax.div(y, 2), lax.rem(y, 2), 0]

    def column(p, z):
        return view.at[lax.div(z, 2), lax.rem(z, 2), :, p, 1]

    for p in range(2):
        for o in FAR[:7]:
            y, z = around(me.y, o, 8), around(me.z, o, 8)
            send(row(p, y), ta_ref.at[p, me.y], ssem.at[0], rsem.at[p], me.at(y=y))
            send(column(p, z), tb_ref.at[p, me.z], ssem.at[1], rsem.at[4 + p], me.at(z=z))
        pltpu.make_async_copy(row(p, me.y), ta_ref.at[p, me.y], lsem.at[p]).start()
        pltpu.make_async_copy(column(p, me.z), tb_ref.at[p, me.z], lsem.at[3 + p]).start()


def orders_second(me, ta_ref, tb_ref, r_ref, ssem, gsem, rsem, lsem):
    here_a, here_b = r_ref.at[me.z, :, me.c], r_ref.at[me.y, :, me.c]
    to_a, to_b = 2 + me.c, 3 - me.c
    for p in range(2):
        settle(ta_ref.at[0, 0], lsem.at[p])
        settle(ta_ref.at[0, 0:7], rsem.at[p])
        settle(tb_ref.at[0, 0], lsem.at[3 + p])
        settle(tb_ref.at[0, 0:7], rsem.at[4 + p])
        for h in range(4):
            z = lax.rem(lax.div(me.z, 2) + h, 4) * 2 + p
            y = lax.rem(lax.div(me.y, 2) + h, 4) * 2 + p
            part_a, part_b = ta_ref.at[p, :, lax.div(z, 2)], tb_ref.at[p, :, lax.div(y, 2)]

            @pl.when(jnp.logical_or(z != me.z, me.c == 1))
            def _():
                send(part_a, here_a, ssem.at[to_a], gsem.at[me.z], me.at(z=z, c=0))

            @pl.when(jnp.logical_or(y != me.y, me.c == 0))
            def _():
                send(part_b, here_b, ssem.at[to_b], gsem.at[me.y], me.at(y=y, c=1))

            @pl.when(jnp.logical_and(z == me.z, me.c == 0))
            def _():
                pltpu.make_async_copy(part_a, here_a, lsem.at[2]).start()

            @pl.when(jnp.logical_and(y == me.y, me.c == 1))
            def _():
                pltpu.make_async_copy(part_b, here_b, lsem.at[2]).start()


def orders_third(me, r_ref, perm_ref, p_ref, q_ref, gsem, lsem, xs, xr):
    for o in NEAR:
        g = around(me.major, o, 8)
        if o == 0:
            settle(r_ref.at[0, :, 0], lsem.at[2])
            settle(r_ref.at[0, :, 0], gsem.at[g])
        else:
            settle(r_ref.at[0], gsem.at[g])
        out = dot(perm_ref[...], r_ref[g].reshape(256, 128)).astype(BF)
        at = pl.ds(pl.multiple_of(g * 64, 64), 64)
        for s in range(4):
            p_ref[s, at, :] = out[s * 64 : (s + 1) * 64]
        for k in (2, 1, 3):
            x = around(me.x, k, 4)
            send(p_ref.at[x, at], q_ref.at[me.x, at], xs, xr, me.at(x=x))
        q_ref[me.x, at, :] = p_ref[me.x, at, :]


def lat_sent(t_ref, ssem):
    settle(t_ref.at[0:7], ssem.at[0])
    settle(t_ref.at[0:7], ssem.at[1])
    settle(t_ref.at[0:7], ssem.at[2])
    settle(t_ref, ssem.at[3])


def grid_first(me, ret_ref, p_ref, xs, gsem):
    for o in FAR:
        g = around(me.major, o, 8)
        at = pl.ds(pl.multiple_of(g * 64, 64), 64)
        for k in (2, 1, 3):
            x = around(me.x, k, 4)
            send(ret_ref.at[x, at], p_ref.at[me.x, at], xs, gsem.at[g], me.at(x=x))
    p_ref[me.x] = ret_ref[me.x]


def grid_second(me, p_ref, perm_ref, s_ref, t_ref, ssem, rsem, gsem, lsem):
    here = t_ref.at[me.c, me.major]
    for o in FAR:
        g = around(me.major, o, 8)
        at = pl.ds(pl.multiple_of(g * 64, 64), 64)
        settle(p_ref.at[0:3, 0:64], gsem.at[g])
        rows = jnp.concatenate([p_ref[s, at, :] for s in range(4)], axis=0)
        s_ref[g] = dot(perm_ref[...], rows, TN).astype(BF).reshape(8, 2, 16, 128)
        z, y = jnp.where(me.c == 0, g, me.z), jnp.where(me.c == 0, me.y, g)
        other = 1 - me.c
        send(s_ref.at[g, :, other], here, ssem.at[3], rsem.at[3], me.at(z=z, y=y, c=other))
        if o == 0:
            pltpu.make_async_copy(s_ref.at[g, :, me.c], here, lsem.at[0]).start()
        else:
            send(s_ref.at[g, :, me.c], here, ssem.at[2], rsem.at[2], me.at(z=z, y=y))


def grid_third(me, t_ref, r_ref, ssem, rsem, lsem):
    settle(t_ref.at[0, 0], lsem.at[0])
    settle(t_ref.at[0, 0:7], rsem.at[2])
    settle(t_ref.at[0], rsem.at[3])
    here_a, here_b = r_ref.at[:, me.y, 0], r_ref.at[me.z, :, 1]
    for o in FAR[:7]:
        y, z = around(me.y, o, 8), around(me.z, o, 8)
        send(t_ref.at[0, :, y], here_a, ssem.at[0], rsem.at[0], me.at(y=y))
        send(t_ref.at[1, :, z], here_b, ssem.at[1], rsem.at[1], me.at(z=z))
    pltpu.make_async_copy(t_ref.at[0, :, me.y], here_a, lsem.at[1]).start()
    pltpu.make_async_copy(t_ref.at[1, :, me.z], here_b, lsem.at[2]).start()


def grid_end(t_ref, rsem, lsem):
    settle(t_ref.at[0, 0], lsem.at[1])
    settle(t_ref.at[0, 0], lsem.at[2])
    settle(t_ref.at[0, 0:7], rsem.at[0])
    settle(t_ref.at[0, 0:7], rsem.at[1])


def x_start(me, src_ref, dst_ref, ssem, rsem, lsem):
    for o in (2, 1, 3):
        x = around(me.x, o, 4)
        send(src_ref.at[x], dst_ref.at[me.x], ssem, rsem, me.at(x=x))
    pltpu.make_async_copy(src_ref.at[me.x], dst_ref.at[me.x], lsem).start()


def x_end(dst_ref, rsem, lsem):
    settle(dst_ref.at[0], lsem)
    settle(dst_ref.at[0:3], rsem)


def whole_kernel(
    slots_ref, logs_ref, mrow_ref, cosv_ref, logsin_ref, band_ref, sine_ref, perm_ref, turn_ref, w_ref, gain_ref, xfield_ref, cfield_ref,
    yfield_ref, spectrum_ref, out_ref, mix_ref, ggain_ref,
    x_ref, cot_ref, y_ref,
    f_ref, mcol_ref, up_ref, low_ref, raw_ref, l_ref, lt_ref, shift_ref, shift_t_ref, w2_ref, w2t_ref, gsend_ref, garr_ref, grows_ref,
    stage_ref, grid_ref, slope_ref, coeff_ref, coeff_t_ref, mixed_ref, flat_ref, pre_ref, grad_ref, spec_ref, ret_ref, ret2_ref,
    s_refs, ta_refs, tb_refs, t_refs, r_refs, p_refs, q_refs,
    sums_ref, v_ref, own_ref, ybuf_ref, piece_ref, zbuf_ref, fin_ref, total_ref,
    ssem, rsem, gsem, lsem, xs, xr, xl, gs, gr,
):
    me = Place()
    other = 1 - me.c
    peers = greet(me)
    lat = lax.axis_index("lat")
    order = slots_ref[lat * NX + me.x]
    m = order.astype(F32)
    mrow = mrow_ref[...]
    half_row = jnp.where(mrow == 0, 0.5, 1.0)
    mcol_ref[...] = jnp.transpose(jnp.broadcast_to(mrow.astype(F32), (128, MODES)))
    split_gain(gain_ref, gsend_ref)
    long_tables(mcol_ref, f_ref)

    sines = band_ref[pl.ds(lat, 1), :]
    to_rows(xfield_ref, x_ref)
    g = dot(f_ref[...], x_ref[...], NT) * sines
    pack_blocks(g, perm_ref, s_refs.at[0], stage_ref)
    pl.semaphore_wait(pltpu.get_barrier_semaphore(), peers)

    def xlinks(i):
        return xs.at[i], xr.at[i], xl.at[i]

    def begin(i):
        orders_first(me, s_refs.at[i], ta_refs.at[i // 2], tb_refs.at[i // 2], ssem.at[i], rsem.at[i], lsem.at[i])

    def carry_on(i):
        refs = ta_refs.at[i // 2], tb_refs.at[i // 2], r_refs.at[i]
        orders_second(me, *refs, ssem.at[i], gsem.at[i], rsem.at[i], lsem.at[i])
        refs = r_refs.at[i], turn_ref, p_refs.at[i], q_refs.at[i // 2]
        orders_third(me, *refs, gsem.at[i], lsem.at[i], xs.at[i], xr.at[i])

    def back_on(i):
        refs = p_refs.at[i], turn_ref, s_refs.at[i], t_refs.at[i // 2]
        grid_second(me, *refs, ssem.at[i], rsem.at[i], gsem.at[i], lsem.at[i])

    def back_out(i):
        grid_third(me, t_refs.at[i // 2], r_refs.at[i], ssem.at[i], rsem.at[i], lsem.at[i])

    def back_end(i):
        grid_end(t_refs.at[i // 2], rsem.at[i], lsem.at[i])

    begin(0)
    for o in range(1, 4):
        x = around(me.x, o, 4)
        send(gsend_ref, garr_ref.at[me.x], xs.at[6], xr.at[6], me.at(x=x))
    garr_ref[me.x] = gsend_ref[...]
    to_rows(cfield_ref, cot_ref)
    weights = w_ref[...].astype(F32)
    mixing_weights(weights, w2_ref)
    mixing_weights(jnp.transpose(weights), w2t_ref)
    carry = legendre_start(m, logs_ref[order], logsin_ref[me.c], up_ref, low_ref)
    legendre_steps(0, MODES // RENEW, carry, cosv_ref[me.c], up_ref, low_ref, raw_ref)
    legendre_end(order, raw_ref, l_ref, lt_ref, shift_ref, shift_t_ref)
    carry_on(0)
    settle(garr_ref.at[0:3], xr.at[6])
    gain_rows(shift_ref, garr_ref, grows_ref)
    settle(q_refs.at[0, 0:3], xr.at[0])

    coeff_ref[...] = dot(l_ref[...], flat(q_refs.at[0])).astype(BF)
    mixed_ref[...] = dot(coeff_ref[...], w2_ref[...]).astype(BF)
    flat_ref[...] = (mixed_ref[...].astype(F32) * grows_ref[...]).astype(BF)
    split_lanes(dot(lt_ref[...], flat_ref[...]), None, ret_ref)
    grid_first(me, ret_ref, p_refs.at[1], xs.at[1], gsem.at[1])
    back_on(1)
    back_out(1)
    for x in range(NX):
        cols = slice(x * 128, (x + 1) * 128)
        spec_ref[x] = jnp.transpose(flat_ref[:, cols].astype(F32)).astype(BF)
        coeff_t_ref[cols, :] = jnp.transpose(coeff_ref[:, cols].astype(F32)).astype(BF)
    x_start(me, spec_ref, spectrum_ref, *xlinks(4))
    back_end(1)

    unpack_blocks(r_refs.at[1], perm_ref, half_row, grid_ref)
    middle(grid_ref, x_ref, cot_ref, f_ref, y_ref, slope_ref)
    mcol = mcol_ref[...]
    half_col = jnp.where(jnp.concatenate([mcol, mcol], axis=1) == 0.0, 0.5, 1.0)
    half_col = jnp.concatenate([half_col, half_col], axis=0)
    g = dot(f_ref[...], slope_ref[...], NT) * half_col
    pack_blocks(g, perm_ref, s_refs.at[2], stage_ref)
    begin(2)
    to_field(y_ref, yfield_ref)
    carry_on(2)
    settle(q_refs.at[1, 0:3], xr.at[2])

    grad_ref[...] = dot(l_ref[...], flat(q_refs.at[1]))
    pre_ref[...] = (grad_ref[...] * grows_ref[...]).astype(BF)
    back = dot(pre_ref[...], w2t_ref[...]).astype(BF)
    split_lanes(dot(lt_ref[...], back), sine_ref[me.c], ret2_ref)
    grid_first(me, ret2_ref, p_refs.at[3], xs.at[3], gsem.at[3])
    gain_sums(grad_ref, mixed_ref, shift_t_ref, sums_ref)
    mix_sums(coeff_t_ref, pre_ref, sums_ref)
    x_start(me, sums_ref, v_ref, *xlinks(5))
    back_on(3)
    back_out(3)
    x_end(v_ref, xr.at[5], xl.at[5])
    own_ref[...] = sum(v_ref[x].astype(F32) for x in range(NX)).reshape(2, 8, 24, 128)
    for o in FAR:
        y = around(me.y, o, 8)
        if o > 0:
            send(own_ref.at[me.c, y], ybuf_ref.at[me.c, me.y], gs.at[0], gr.at[0], me.at(y=y))
        send(own_ref.at[other, y], ybuf_ref.at[me.c, me.y], gs.at[1], gr.at[1], me.at(y=y, c=other))
    ybuf_ref[me.c, me.y] = own_ref[me.c, me.y]
    settle(ybuf_ref.at[0, 0:7], gr.at[0])
    settle(ybuf_ref.at[0], gr.at[1])
    piece_ref[...] = jnp.sum(ybuf_ref[0] + ybuf_ref[1], axis=0)
    for o in range(1, 8):
        z = around(me.z, o, 8)
        send(piece_ref, zbuf_ref.at[me.z], gs.at[2], gr.at[2], me.at(z=z))
    zbuf_ref[me.z] = piece_ref[...]
    settle(zbuf_ref.at[0:7], gr.at[2])
    fin_ref[...] = jnp.sum(zbuf_ref[...], axis=0)
    for o in range(8):
        y = around(me.y, o, 8)
        if o > 0:
            send(fin_ref, total_ref.at[me.c, me.y], gs.at[3], gr.at[3], me.at(y=y))
        send(fin_ref, total_ref.at[me.c, me.y], gs.at[4], gr.at[4], me.at(y=y, c=other))
    total_ref[me.c, me.y] = fin_ref[...]
    back_end(3)

    unpack_blocks(r_refs.at[3], perm_ref, None, grid_ref)
    last(grid_ref, cot_ref, f_ref, out_ref)
    settle(total_ref.at[0, 0:7], gr.at[3])
    settle(total_ref.at[0], gr.at[4])
    mix = total_ref[0].reshape(192, 128)[0:128] * (1.0 / MODES)
    mix_ref[...] = jnp.transpose(jnp.concatenate([mix[:, :CL], mix[:, CL:]], axis=0))
    gain = jnp.concatenate([total_ref[0].reshape(192, 128)[128:192], total_ref[1].reshape(192, 128)], axis=0)
    gain = jnp.concatenate([gain[:, :CL], gain[:, CL:]], axis=0) * (1.0 / math.sqrt(MODES))
    ggain_ref[...] = jnp.transpose(gain)

    for i in range(4):
        lat_sent(t_refs.at[0, 0], ssem.at[i])
    x_end(spectrum_ref, xr.at[4], xl.at[4])
    for i in range(5):
        settle(p_refs.at[0, 0:3], xs.at[i])
    settle(v_ref.at[0:3], xs.at[5])
    settle(garr_ref.at[0:3], xs.at[6])
    settle(ybuf_ref.at[0, 0:7], gs.at[0])
    settle(ybuf_ref.at[0], gs.at[1])
    settle(zbuf_ref.at[0:7], gs.at[2])
    settle(total_ref.at[0, 0:7], gs.at[3])
    settle(total_ref.at[0], gs.at[4])


VM = pl.BlockSpec(memory_space=pltpu.VMEM)
SM = pl.BlockSpec(memory_space=pltpu.SMEM)


def whole(*operands):
    scratch = [
        *[((256, NLON), BF)] * 3,
        ((2 * MODES, NLON), BF), ((MODES, 128), F32), ((MODES, 128), F32), ((MODES, 128), F32), ((MODES * 4, 128), F32),
        *[((512, 512), BF)] * 6, ((512, 128), BF), ((4, 512, 128), BF),
        ((512, 512), F32),
        ((4, 512, 128), BF), ((256, 1024), BF), ((256, NLON), BF), ((512, 512), BF), ((512, 512), BF), ((512, 512), BF), ((512, 512), BF),
        ((512, 512), BF), ((512, 512), F32), ((4, 128, 512), BF), ((4, 512, 128), BF), ((4, 512, 128), BF),
        ((4, NZ, NY, NC, 16, 128), BF), ((2, 2, 8, 4, 16, 128), BF), ((2, 2, 8, 4, 16, 128), BF), ((2, 2, 8, 8, 16, 128), BF),
        ((4, NZ, NY, NC, 16, 128), BF),
        ((4, 4, 512, 128), BF), ((2, 4, 512, 128), BF),
        ((4, 384, 128), BF), ((4, 384, 128), BF), ((2, 8, 24, 128), F32), ((2, 8, 24, 128), F32),
        ((24, 128), F32), ((8, 24, 128), F32), ((24, 128), F32), ((2, 8, 24, 128), F32),
    ]
    sems = [(4, 4), (4, 6), (4, 8), (4, 5), (7,), (7,), (7,), (5,), (5,)]
    outs = [((CL, JL, NLON), BF), ((4, 128, 512), BF), ((256, NLON), BF), ((64, 256), F32), ((64, 512), F32)]
    return pl.pallas_call(
        whole_kernel,
        out_shape=tuple(jax.ShapeDtypeStruct(*o) for o in outs),
        in_specs=[SM, SM] + [VM] * (len(operands) - 2),
        out_specs=tuple(VM for _ in outs),
        scratch_shapes=[pltpu.VMEM(*s) for s in scratch] + [pltpu.SemaphoreType.DMA(s) for s in sems],
        compiler_params=pltpu.CompilerParams(vmem_limit_bytes=VMEM_BYTES, collective_id=0, has_side_effects=True),
        name="whole",
    )(*operands)


def finish_kernel(y_in, spec_in, grad_in, mix_in, gain_in, y_out, spec_out, grad_out, mix_out, gain_out):
    y_out[...] = y_in[...]
    spec_out[...] = spec_in[...]
    to_field(grad_in, grad_out)
    mix_out[...] = mix_in[...]
    gain_out[...] = gain_in[...]


def finish(y, spectrum, grad, mix, gain):
    outs = [((CL, JL, NLON), BF), ((4, 128, 512), BF), ((CL, JL, NLON), BF), ((64, 256), F32), ((64, 512), F32)]
    return pl.pallas_call(
        finish_kernel,
        out_shape=tuple(jax.ShapeDtypeStruct(*o) for o in outs),
        in_specs=[VM] * 5,
        out_specs=(VM,) * 5,
        compiler_params=pltpu.CompilerParams(vmem_limit_bytes=VMEM_BYTES),
        name="finish",
    )(y, spectrum, grad, mix, gain)


def one_hot(rows):
    out = np.zeros((rows.size, rows.size), np.float32)
    out[np.arange(rows.size), rows] = 1.0
    return jnp.asarray(out, BF)


def body(grid_field, order_slots, mix_weight, degree_gain, cotangent):
    d, s, j = np.meshgrid(np.arange(32), np.arange(4), np.arange(4), indexing="ij")
    perm = one_hot((j * 128 + d * 4 + s).reshape(-1))
    s, e, j = np.meshgrid(np.arange(4), np.arange(16), np.arange(4), indexing="ij")
    turn = one_hot((e * 16 + s * 4 + j).reshape(-1))
    theta = math.pi * (np.arange(NLAT) + 0.5) / NLAT
    both = np.stack([theta, theta.reshape(8, 8, 8).transpose(1, 0, 2).reshape(-1)])
    cosv = jnp.asarray(np.cos(both).reshape(2, 4, 128), F32)
    logsin = jnp.asarray(np.log(np.sin(both)).reshape(2, 4, 128), F32)
    band = jnp.asarray(np.repeat(np.sin(theta).reshape(128, JL), CL, axis=1), F32)
    sine_col = jnp.asarray(np.repeat(np.sin(both).reshape(2, NLAT, 1), 128, axis=2), F32)
    n = np.arange(1, MODES)
    logs = jnp.asarray(np.concatenate([[0.0], np.cumsum(np.log((2.0 * n - 1.0) / (2.0 * n)))]), F32)
    out, spectrum, grad, mix, gain = whole(
        order_slots, logs, order_slots.reshape(1, MODES), cosv, logsin, band, sine_col, perm, turn,
        mix_weight, degree_gain, grid_field, cotangent,
    )
    out, spectrum, grad, mix, gain = finish(out, spectrum, grad, mix, gain)
    return out, spectrum.reshape(4, 2, CL, MODES), grad, mix.T, gain


def solution(mesh):
    placed = (P("ch", "lat", None), P(), P(), P("ch", None), P("ch", "lat", None))
    return jax.shard_map(
        body,
        mesh=mesh,
        in_specs=placed,
        out_specs=(
            P("ch", "lat", None),
            P("lat", None, "ch", None),
            P("ch", "lat", None),
            P(None, "ch"),
            P("ch", None),
        ),
        check_vma=False,
    )
```

```python
import math

import jax
import jax.numpy as jnp
import numpy as np
from jax import lax
from jax.experimental import pallas as pl
from jax.experimental.pallas import tpu as pltpu
from jax.sharding import PartitionSpec as P

MESH = pl.DeviceIdType.MESH
BF, F32 = jnp.bfloat16, jnp.float32
CL, JL, NLON = 64, 4, 1440
NZ, NY, NC, NX = 8, 8, 2, 4
NLAT, MODES = 512, 512
RENEW = 32
VMEM_BYTES = 56 * 1024 * 1024
NN = (((1,), (0,)), ((), ()))
NT = (((1,), (1,)), ((), ()))
TN = (((0,), (0,)), ((), ()))


def dot(a, b, dims=NN):
    return lax.dot_general(a, b, dims, preferred_element_type=F32)


def half_angle(steps):
    turns = jnp.floor(steps * (1.0 / NLON) + 0.5)
    t = (steps - turns * NLON) * (math.pi / NLON)
    u = t * t
    s = t * (1.0 + u * (-1.0 / 6 + u * (1.0 / 120 + u * (-1.0 / 5040 + u * (1.0 / 362880 + u * (-1.0 / 39916800))))))
    c = 1.0 + u * (-0.5 + u * (1.0 / 24 + u * (-1.0 / 720 + u * (1.0 / 40320 + u * (-1.0 / 3628800 + u * (1.0 / 479001600))))))
    return 1.0 - 2.0 * s * s, 2.0 * s * c


def long_tables(mcol_ref, f_ref):
    def long_rows(i, carry):
        rows = pl.ds(pl.multiple_of(i * 64, 64), 64)
        lower = pl.ds(pl.multiple_of(i * 64 + MODES, 64), 64)
        mc = mcol_ref[rows, :]
        lane = lax.broadcasted_iota(jnp.int32, (64, 128), 1).astype(F32)
        cb, sb = half_angle(mc * lane)
        ca, sa = half_angle(mc * (lane * 128.0))
        cb, sb = cb * math.sqrt(2.0 / NLON), sb * math.sqrt(2.0 / NLON)
        for a in range(12):
            width = min(128, NLON - a * 128)
            cav = jnp.broadcast_to(ca[:, a : a + 1], (64, 128))
            sav = jnp.broadcast_to(sa[:, a : a + 1], (64, 128))
            f_ref[rows, a * 128 : a * 128 + width] = (cav * cb - sav * sb).astype(BF)[:, :width]
            f_ref[lower, a * 128 : a * 128 + width] = (-(sav * cb + cav * sb)).astype(BF)[:, :width]
        return carry

    lax.fori_loop(0, 8, long_rows, 0)


def legendre_start(m, logs, logsin, up_ref, low_ref):
    k = lax.broadcasted_iota(jnp.int32, (MODES, 128), 0).astype(F32)
    degree = k + (m + 1.0)
    upper = jnp.sqrt((4.0 * degree * degree - 1.0) / (degree * degree - m * m))
    below = degree - 1.0
    lower = jnp.sqrt((below * below - m * m) / jnp.maximum(4.0 * below * below - 1.0, 1.0))
    up_ref[...] = upper
    low_ref[...] = upper * lower
    start = 0.5 * (jnp.log(jnp.full((4, 128), m + 0.5, F32)) + logs) + m * logsin
    zero = jnp.zeros((4, 128), F32)
    return zero, zero + 1.0, start


def legendre_steps(first, last, carry, cosv, up_ref, low_ref, raw_ref):
    def block(b, carry):
        previous, current, scale = carry
        factor = jnp.exp(0.5 * scale)
        for offset in range(RENEW):
            step = b * RENEW + offset
            raw_ref[pl.ds(pl.multiple_of(step * 4, 4), 4), :] = current * factor * factor
            ua = jnp.broadcast_to(up_ref[pl.ds(step, 1), :], (4, 128)) * cosv
            lb = jnp.broadcast_to(low_ref[pl.ds(step, 1), :], (4, 128))
            previous, current = current, ua * current - lb * previous
        biggest = jnp.maximum(jnp.abs(previous), jnp.abs(current))
        shift = jnp.log(biggest)
        rescale = jnp.exp(-shift)
        return previous * rescale, current * rescale, scale + shift

    return lax.fori_loop(first, last, block, carry)


def legendre_end(order, raw_ref, l_ref, lt_ref, shift_ref, shift_t_ref):
    live = lax.broadcasted_iota(jnp.int32, (MODES, 128), 0) < MODES - order
    for g in range(4):
        part = raw_ref[pl.ds(g, MODES, stride=4), :]
        part = jnp.where(live, part, 0.0) * math.sqrt(math.pi / NLAT)
        l_ref[:, g * 128 : (g + 1) * 128] = part.astype(BF)
        lt_ref[g * 128 : (g + 1) * 128, :] = jnp.transpose(part).astype(BF)
    k = lax.broadcasted_iota(jnp.int32, (MODES, MODES), 0)
    l = lax.broadcasted_iota(jnp.int32, (MODES, MODES), 1)
    shift_ref[...] = jnp.where(l - k == order, 1.0, 0.0).astype(BF)
    shift_t_ref[...] = jnp.where(k - l == order, 1.0, 0.0).astype(BF)


def pack_blocks(g, perm_ref, s_ref, stage_ref):
    for j in range(JL):
        cols = slice(j * CL, (j + 1) * CL)
        stage_ref[j] = jnp.concatenate([g[:MODES, cols], g[MODES:, cols]], axis=1).astype(BF)
    for g in range(4):
        rows = jnp.concatenate([stage_ref[j, g * 128 : (g + 1) * 128, :] for j in range(JL)], axis=0)
        s_ref[2 * g : 2 * g + 2] = dot(perm_ref[...], rows).astype(BF).reshape(2, 8, 2, 16, 128)


def unpack_blocks(r_ref, perm_ref, half, grid_ref):
    for g in range(4):
        rows = r_ref[2 * g : 2 * g + 2].reshape(512, 128)
        turned = dot(rows, perm_ref[...], TN)
        for j in range(JL):
            piece = turned[:, j * 128 : (j + 1) * 128]
            if half is not None:
                piece = piece * half[:, g * 128 : (g + 1) * 128]
            piece = piece.astype(BF)
            for r in range(2):
                at = r * MODES + g * 128
                grid_ref[j * CL : (j + 1) * CL, at : at + 128] = piece[r * CL : (r + 1) * CL]


CHUNKS = ((0, 384), (384, 384), (768, 384), (1152, 288))


def to_rows(field_ref, rows_ref):
    for j in range(JL):
        rows_ref[j * CL : (j + 1) * CL, :] = field_ref[:, j, :]


def to_field(rows_ref, field_ref):
    for j in range(JL):
        field_ref[:, j, :] = rows_ref[j * CL : (j + 1) * CL, :]


def middle(grid_ref, x_ref, cot_ref, f_ref, y_ref, slope_ref):
    for first, width in CHUNKS:
        cols = slice(first, first + width)
        v = dot(grid_ref[...], f_ref[:, cols])
        cdf = 0.5 * (1.0 + lax.erf(v * (1.0 / math.sqrt(2.0))))
        y_ref[:, cols] = (x_ref[:, cols].astype(F32) + v * cdf).astype(BF)
        slope = cdf + v * jnp.exp(-0.5 * v * v) * (1.0 / math.sqrt(2.0 * math.pi))
        slope_ref[:, cols] = (cot_ref[:, cols].astype(F32) * slope).astype(BF)


def last(grid_ref, cot_ref, f_ref, out_ref):
    for first, width in CHUNKS:
        cols = slice(first, first + width)
        v = dot(grid_ref[...], f_ref[:, cols])
        out_ref[:, cols] = (cot_ref[:, cols].astype(F32) + v).astype(BF)


def mixing_weights(weights, w2_ref):
    zero = jnp.zeros((CL, CL), F32)
    for x in range(NX):
        slab = weights[x * CL : (x + 1) * CL, :]
        pieces = [slab[:, i * CL : (i + 1) * CL] for i in range(NX)]
        top = jnp.concatenate([a for p in pieces for a in (p, zero)], axis=1)
        low = jnp.concatenate([a for p in pieces for a in (zero, p)], axis=1)
        w2_ref[x * 128 : x * 128 + CL, :] = top.astype(BF)
        w2_ref[x * 128 + CL : (x + 1) * 128, :] = low.astype(BF)


def split_gain(gain_ref, out_ref):
    turned = jnp.transpose(gain_ref[...])
    high = turned.astype(BF).astype(F32)
    out_ref[...] = jnp.concatenate([high, turned - high], axis=1).astype(BF)


def gain_rows(shift_ref, garr_ref, rows_ref):
    both = dot(shift_ref[...], flat(garr_ref))
    for x in range(NX):
        row = both[:, x * 128 : x * 128 + CL] + both[:, x * 128 + CL : (x + 1) * 128]
        rows_ref[:, x * 128 : (x + 1) * 128] = jnp.concatenate([row, row], axis=1)


def gain_sums(grad_ref, mixed_ref, shift_t_ref, sums_ref):
    parts = []
    for x in range(NX):
        cols = slice(x * 128, (x + 1) * 128)
        prod = grad_ref[:, cols] * mixed_ref[:, cols].astype(F32)
        prod = prod[:, :CL] + prod[:, CL:]
        high = prod.astype(BF).astype(F32)
        parts.append(jnp.concatenate([high, prod - high], axis=1).astype(BF))
    both = dot(shift_t_ref[...], jnp.concatenate(parts, axis=1))
    for x in range(NX):
        row = both[:, x * 128 : x * 128 + CL] + both[:, x * 128 + CL : (x + 1) * 128]
        sums_ref[x, 128:384, :] = jnp.concatenate([row[:256], row[256:]], axis=1).astype(BF)


def mix_sums(coeff_t_ref, pre_ref, sums_ref):
    mix = dot(coeff_t_ref[...], pre_ref[...])
    for x in range(NX):
        blocks = []
        for i in range(NX):
            a = mix[i * 128 : i * 128 + CL, x * 128 : x * 128 + CL]
            b = mix[i * 128 + CL : (i + 1) * 128, x * 128 + CL : (x + 1) * 128]
            blocks.append(a + b)
        low = jnp.concatenate([blocks[0], blocks[1]], axis=0)
        high = jnp.concatenate([blocks[2], blocks[3]], axis=0)
        sums_ref[x, 0:128, :] = jnp.concatenate([low, high], axis=1).astype(BF)


def flat(q_ref):
    return jnp.concatenate([q_ref[x] for x in range(NX)], axis=1)


def split_lanes(value, scale, ref):
    for x in range(NX):
        part = value[:, x * 128 : (x + 1) * 128]
        ref[x] = (part if scale is None else part * scale).astype(BF)


class Place:
    def __init__(self):
        lat = lax.axis_index("lat")
        self.x = lax.axis_index("ch")
        self.c = lax.rem(lat, 2)
        self.y = lax.rem(lax.div(lat, 2), 8)
        self.z = lax.div(lat, 16)
        self.major = jnp.where(self.c == 0, self.z, self.y)

    def at(self, z=None, y=None, c=None, x=None):
        z, y = (self.z if z is None else z), (self.y if y is None else y)
        c, x = (self.c if c is None else c), (self.x if x is None else x)
        return ((z * 8 + y) * 2 + c, x)


NEAR = (0, 1, 7, 2, 6, 3, 5, 4)
FAR = (4, 3, 5, 2, 6, 1, 7, 0)


def around(value, step, count):
    return lax.rem(value + step, count)


def send(src, dst, ssem, rsem, target):
    pltpu.make_async_remote_copy(
        src_ref=src, dst_ref=dst, send_sem=ssem, recv_sem=rsem, device_id=target, device_id_type=MESH
    ).start()


def settle(view, sem):
    pltpu.make_async_copy(view, view, sem).wait()


def greet(me):
    barrier = pltpu.get_barrier_semaphore()
    other = 1 - me.c
    targets = [me.at(c=other)]
    for o in range(1, 8):
        targets += [me.at(y=around(me.y, o, 8)), me.at(z=around(me.z, o, 8))]
        targets += [me.at(y=around(me.y, o, 8), c=other), me.at(z=around(me.z, o, 8), c=other)]
    for o in range(1, 4):
        targets.append(me.at(x=around(me.x, o, 4)))
    for target in targets:
        pl.semaphore_signal(barrier, inc=1, device_id=target, device_id_type=MESH)
    return len(targets)


def orders_first(me, s_ref, ta_ref, tb_ref, ssem, rsem, lsem):
    view = s_ref.reshape(4, 2, 4, 2, NC, 16, 128)

    def row(p, y):
        return view.at[:, p, lax.div(y, 2), lax.rem(y, 2), 0]

    def column(p, z):
        return view.at[lax.div(z, 2), lax.rem(z, 2), :, p, 1]

    for p in range(2):
        for o in FAR[:7]:
            y, z = around(me.y, o, 8), around(me.z, o, 8)
            send(row(p, y), ta_ref.at[p, me.y], ssem.at[0], rsem.at[p], me.at(y=y))
            send(column(p, z), tb_ref.at[p, me.z], ssem.at[1], rsem.at[4 + p], me.at(z=z))
        pltpu.make_async_copy(row(p, me.y), ta_ref.at[p, me.y], lsem.at[p]).start()
        pltpu.make_async_copy(column(p, me.z), tb_ref.at[p, me.z], lsem.at[3 + p]).start()


def orders_second(me, ta_ref, tb_ref, r_ref, ssem, gsem, rsem, lsem):
    here_a, here_b = r_ref.at[me.z, :, me.c], r_ref.at[me.y, :, me.c]
    to_a, to_b = 2 + me.c, 3 - me.c
    for p in range(2):
        settle(ta_ref.at[0, 0], lsem.at[p])
        settle(ta_ref.at[0, 0:7], rsem.at[p])
        settle(tb_ref.at[0, 0], lsem.at[3 + p])
        settle(tb_ref.at[0, 0:7], rsem.at[4 + p])
        for h in range(4):
            z = lax.rem(lax.div(me.z, 2) + h, 4) * 2 + p
            y = lax.rem(lax.div(me.y, 2) + h, 4) * 2 + p
            part_a, part_b = ta_ref.at[p, :, lax.div(z, 2)], tb_ref.at[p, :, lax.div(y, 2)]

            @pl.when(jnp.logical_or(z != me.z, me.c == 1))
            def _():
                send(part_a, here_a, ssem.at[to_a], gsem.at[me.z], me.at(z=z, c=0))

            @pl.when(jnp.logical_or(y != me.y, me.c == 0))
            def _():
                send(part_b, here_b, ssem.at[to_b], gsem.at[me.y], me.at(y=y, c=1))

            @pl.when(jnp.logical_and(z == me.z, me.c == 0))
            def _():
                pltpu.make_async_copy(part_a, here_a, lsem.at[2]).start()

            @pl.when(jnp.logical_and(y == me.y, me.c == 1))
            def _():
                pltpu.make_async_copy(part_b, here_b, lsem.at[2]).start()


def orders_third(me, r_ref, perm_ref, p_ref, q_ref, gsem, lsem, xs, xr):
    for o in NEAR:
        g = around(me.major, o, 8)
        if o == 0:
            settle(r_ref.at[0, :, 0], lsem.at[2])
            settle(r_ref.at[0, :, 0], gsem.at[g])
        else:
            settle(r_ref.at[0], gsem.at[g])
        out = dot(perm_ref[...], r_ref[g].reshape(256, 128)).astype(BF)
        at = pl.ds(pl.multiple_of(g * 64, 64), 64)
        for s in range(4):
            p_ref[s, at, :] = out[s * 64 : (s + 1) * 64]
        for k in (2, 1, 3):
            x = around(me.x, k, 4)
            send(p_ref.at[x, at], q_ref.at[me.x, at], xs, xr, me.at(x=x))
        q_ref[me.x, at, :] = p_ref[me.x, at, :]


def lat_sent(t_ref, ssem):
    settle(t_ref.at[0:7], ssem.at[0])
    settle(t_ref.at[0:7], ssem.at[1])
    settle(t_ref.at[0:7], ssem.at[2])
    settle(t_ref, ssem.at[3])


def grid_first(me, ret_ref, p_ref, xs, gsem):
    for o in FAR:
        g = around(me.major, o, 8)
        at = pl.ds(pl.multiple_of(g * 64, 64), 64)
        for k in (2, 1, 3):
            x = around(me.x, k, 4)
            send(ret_ref.at[x, at], p_ref.at[me.x, at], xs, gsem.at[g], me.at(x=x))
    p_ref[me.x] = ret_ref[me.x]


def grid_second(me, p_ref, perm_ref, s_ref, t_ref, ssem, rsem, gsem, lsem):
    here = t_ref.at[me.c, me.major]
    for o in FAR:
        g = around(me.major, o, 8)
        at = pl.ds(pl.multiple_of(g * 64, 64), 64)
        settle(p_ref.at[0:3, 0:64], gsem.at[g])
        rows = jnp.concatenate([p_ref[s, at, :] for s in range(4)], axis=0)
        s_ref[g] = dot(perm_ref[...], rows, TN).astype(BF).reshape(8, 2, 16, 128)
        z, y = jnp.where(me.c == 0, g, me.z), jnp.where(me.c == 0, me.y, g)
        other = 1 - me.c
        send(s_ref.at[g, :, other], here, ssem.at[3], rsem.at[3], me.at(z=z, y=y, c=other))
        if o == 0:
            pltpu.make_async_copy(s_ref.at[g, :, me.c], here, lsem.at[0]).start()
        else:
            send(s_ref.at[g, :, me.c], here, ssem.at[2], rsem.at[2], me.at(z=z, y=y))


def grid_third(me, t_ref, r_ref, ssem, rsem, lsem):
    settle(t_ref.at[0, 0], lsem.at[0])
    settle(t_ref.at[0, 0:7], rsem.at[2])
    settle(t_ref.at[0], rsem.at[3])
    here_a, here_b = r_ref.at[:, me.y, 0], r_ref.at[me.z, :, 1]
    for o in FAR[:7]:
        y, z = around(me.y, o, 8), around(me.z, o, 8)
        send(t_ref.at[0, :, y], here_a, ssem.at[0], rsem.at[0], me.at(y=y))
        send(t_ref.at[1, :, z], here_b, ssem.at[1], rsem.at[1], me.at(z=z))
    pltpu.make_async_copy(t_ref.at[0, :, me.y], here_a, lsem.at[1]).start()
    pltpu.make_async_copy(t_ref.at[1, :, me.z], here_b, lsem.at[2]).start()


def grid_end(t_ref, rsem, lsem):
    settle(t_ref.at[0, 0], lsem.at[1])
    settle(t_ref.at[0, 0], lsem.at[2])
    settle(t_ref.at[0, 0:7], rsem.at[0])
    settle(t_ref.at[0, 0:7], rsem.at[1])


def x_start(me, src_ref, dst_ref, ssem, rsem, lsem):
    for o in (2, 1, 3):
        x = around(me.x, o, 4)
        send(src_ref.at[x], dst_ref.at[me.x], ssem, rsem, me.at(x=x))
    pltpu.make_async_copy(src_ref.at[me.x], dst_ref.at[me.x], lsem).start()


def x_end(dst_ref, rsem, lsem):
    settle(dst_ref.at[0], lsem)
    settle(dst_ref.at[0:3], rsem)


def whole_kernel(
    slots_ref, logs_ref, mrow_ref, cosv_ref, logsin_ref, band_ref, sine_ref, perm_ref, turn_ref, w_ref, gain_ref, xfield_ref, cfield_ref,
    yfield_ref, spectrum_ref, out_ref, mix_ref, ggain_ref,
    x_ref, cot_ref, y_ref,
    f_ref, mcol_ref, up_ref, low_ref, raw_ref, l_ref, lt_ref, shift_ref, shift_t_ref, w2_ref, w2t_ref, gsend_ref, garr_ref, grows_ref,
    stage_ref, grid_ref, slope_ref, coeff_ref, coeff_t_ref, mixed_ref, flat_ref, pre_ref, grad_ref, spec_ref, ret_ref, ret2_ref,
    s_refs, ta_refs, tb_refs, t_refs, r_refs, p_refs, q_refs,
    sums_ref, v_ref, own_ref, ybuf_ref, piece_ref, zbuf_ref, fin_ref, total_ref,
    ssem, rsem, gsem, lsem, xs, xr, xl, gs, gr,
):
    me = Place()
    other = 1 - me.c
    peers = greet(me)
    lat = lax.axis_index("lat")
    order = slots_ref[lat * NX + me.x]
    m = order.astype(F32)
    mrow = mrow_ref[...]
    half_row = jnp.where(mrow == 0, 0.5, 1.0)
    mcol_ref[...] = jnp.transpose(jnp.broadcast_to(mrow.astype(F32), (128, MODES)))
    split_gain(gain_ref, gsend_ref)
    long_tables(mcol_ref, f_ref)

    sines = band_ref[pl.ds(lat, 1), :]
    to_rows(xfield_ref, x_ref)
    g = dot(f_ref[...], x_ref[...], NT) * sines
    pack_blocks(g, perm_ref, s_refs.at[0], stage_ref)
    pl.semaphore_wait(pltpu.get_barrier_semaphore(), peers)

    def xlinks(i):
        return xs.at[i], xr.at[i], xl.at[i]

    def begin(i):
        orders_first(me, s_refs.at[i], ta_refs.at[i // 2], tb_refs.at[i // 2], ssem.at[i], rsem.at[i], lsem.at[i])

    def carry_on(i):
        refs = ta_refs.at[i // 2], tb_refs.at[i // 2], r_refs.at[i]
        orders_second(me, *refs, ssem.at[i], gsem.at[i], rsem.at[i], lsem.at[i])
        refs = r_refs.at[i], turn_ref, p_refs.at[i], q_refs.at[i // 2]
        orders_third(me, *refs, gsem.at[i], lsem.at[i], xs.at[i], xr.at[i])

    def back_on(i):
        refs = p_refs.at[i], turn_ref, s_refs.at[i], t_refs.at[i // 2]
        grid_second(me, *refs, ssem.at[i], rsem.at[i], gsem.at[i], lsem.at[i])

    def back_out(i):
        grid_third(me, t_refs.at[i // 2], r_refs.at[i], ssem.at[i], rsem.at[i], lsem.at[i])

    def back_end(i):
        grid_end(t_refs.at[i // 2], rsem.at[i], lsem.at[i])

    begin(0)
    for o in range(1, 4):
        x = around(me.x, o, 4)
        send(gsend_ref, garr_ref.at[me.x], xs.at[6], xr.at[6], me.at(x=x))
    garr_ref[me.x] = gsend_ref[...]
    to_rows(cfield_ref, cot_ref)
    weights = w_ref[...].astype(F32)
    mixing_weights(weights, w2_ref)
    mixing_weights(jnp.transpose(weights), w2t_ref)
    carry = legendre_start(m, logs_ref[order], logsin_ref[me.c], up_ref, low_ref)
    legendre_steps(0, MODES // RENEW, carry, cosv_ref[me.c], up_ref, low_ref, raw_ref)
    legendre_end(order, raw_ref, l_ref, lt_ref, shift_ref, shift_t_ref)
    carry_on(0)
    settle(garr_ref.at[0:3], xr.at[6])
    gain_rows(shift_ref, garr_ref, grows_ref)
    settle(q_refs.at[0, 0:3], xr.at[0])

    coeff_ref[...] = dot(l_ref[...], flat(q_refs.at[0])).astype(BF)
    mixed_ref[...] = dot(coeff_ref[...], w2_ref[...]).astype(BF)
    flat_ref[...] = (mixed_ref[...].astype(F32) * grows_ref[...]).astype(BF)
    split_lanes(dot(lt_ref[...], flat_ref[...]), None, ret_ref)
    grid_first(me, ret_ref, p_refs.at[1], xs.at[1], gsem.at[1])
    back_on(1)
    back_out(1)
    for x in range(NX):
        cols = slice(x * 128, (x + 1) * 128)
        spec_ref[x] = jnp.transpose(flat_ref[:, cols].astype(F32)).astype(BF)
        coeff_t_ref[cols, :] = jnp.transpose(coeff_ref[:, cols].astype(F32)).astype(BF)
    x_start(me, spec_ref, spectrum_ref, *xlinks(4))
    back_end(1)

    unpack_blocks(r_refs.at[1], perm_ref, half_row, grid_ref)
    middle(grid_ref, x_ref, cot_ref, f_ref, y_ref, slope_ref)
    mcol = mcol_ref[...]
    half_col = jnp.where(jnp.concatenate([mcol, mcol], axis=1) == 0.0, 0.5, 1.0)
    half_col = jnp.concatenate([half_col, half_col], axis=0)
    g = dot(f_ref[...], slope_ref[...], NT) * half_col
    pack_blocks(g, perm_ref, s_refs.at[2], stage_ref)
    begin(2)
    to_field(y_ref, yfield_ref)
    carry_on(2)
    settle(q_refs.at[1, 0:3], xr.at[2])

    grad_ref[...] = dot(l_ref[...], flat(q_refs.at[1]))
    pre_ref[...] = (grad_ref[...] * grows_ref[...]).astype(BF)
    back = dot(pre_ref[...], w2t_ref[...]).astype(BF)
    split_lanes(dot(lt_ref[...], back), sine_ref[me.c], ret2_ref)
    grid_first(me, ret2_ref, p_refs.at[3], xs.at[3], gsem.at[3])
    gain_sums(grad_ref, mixed_ref, shift_t_ref, sums_ref)
    mix_sums(coeff_t_ref, pre_ref, sums_ref)
    x_start(me, sums_ref, v_ref, *xlinks(5))
    back_on(3)
    back_out(3)
    x_end(v_ref, xr.at[5], xl.at[5])
    own_ref[...] = sum(v_ref[x].astype(F32) for x in range(NX)).reshape(2, 8, 24, 128)
    for o in FAR:
        y = around(me.y, o, 8)
        if o > 0:
            send(own_ref.at[me.c, y], ybuf_ref.at[me.c, me.y], gs.at[0], gr.at[0], me.at(y=y))
        send(own_ref.at[other, y], ybuf_ref.at[me.c, me.y], gs.at[1], gr.at[1], me.at(y=y, c=other))
    ybuf_ref[me.c, me.y] = own_ref[me.c, me.y]
    settle(ybuf_ref.at[0, 0:7], gr.at[0])
    settle(ybuf_ref.at[0], gr.at[1])
    piece_ref[...] = jnp.sum(ybuf_ref[0] + ybuf_ref[1], axis=0)
    for o in range(1, 8):
        z = around(me.z, o, 8)
        send(piece_ref, zbuf_ref.at[me.z], gs.at[2], gr.at[2], me.at(z=z))
    zbuf_ref[me.z] = piece_ref[...]
    settle(zbuf_ref.at[0:7], gr.at[2])
    fin_ref[...] = jnp.sum(zbuf_ref[...], axis=0)
    for o in range(8):
        y = around(me.y, o, 8)
        if o > 0:
            send(fin_ref, total_ref.at[me.c, me.y], gs.at[3], gr.at[3], me.at(y=y))
        send(fin_ref, total_ref.at[me.c, me.y], gs.at[4], gr.at[4], me.at(y=y, c=other))
    total_ref[me.c, me.y] = fin_ref[...]
    back_end(3)

    unpack_blocks(r_refs.at[3], perm_ref, None, grid_ref)
    last(grid_ref, cot_ref, f_ref, out_ref)
    settle(total_ref.at[0, 0:7], gr.at[3])
    settle(total_ref.at[0], gr.at[4])
    mix = total_ref[0].reshape(192, 128)[0:128] * (1.0 / MODES)
    mix_ref[...] = jnp.transpose(jnp.concatenate([mix[:, :CL], mix[:, CL:]], axis=0))
    gain = jnp.concatenate([total_ref[0].reshape(192, 128)[128:192], total_ref[1].reshape(192, 128)], axis=0)
    gain = jnp.concatenate([gain[:, :CL], gain[:, CL:]], axis=0) * (1.0 / math.sqrt(MODES))
    ggain_ref[...] = jnp.transpose(gain)

    for i in range(4):
        lat_sent(t_refs.at[0, 0], ssem.at[i])
    x_end(spectrum_ref, xr.at[4], xl.at[4])
    for i in range(5):
        settle(p_refs.at[0, 0:3], xs.at[i])
    settle(v_ref.at[0:3], xs.at[5])
    settle(garr_ref.at[0:3], xs.at[6])
    settle(ybuf_ref.at[0, 0:7], gs.at[0])
    settle(ybuf_ref.at[0], gs.at[1])
    settle(zbuf_ref.at[0:7], gs.at[2])
    settle(total_ref.at[0, 0:7], gs.at[3])
    settle(total_ref.at[0], gs.at[4])


VM = pl.BlockSpec(memory_space=pltpu.VMEM)
SM = pl.BlockSpec(memory_space=pltpu.SMEM)


def whole(*operands):
    scratch = [
        *[((256, NLON), BF)] * 3,
        ((2 * MODES, NLON), BF), ((MODES, 128), F32), ((MODES, 128), F32), ((MODES, 128), F32), ((MODES * 4, 128), F32),
        *[((512, 512), BF)] * 6, ((512, 128), BF), ((4, 512, 128), BF),
        ((512, 512), F32),
        ((4, 512, 128), BF), ((256, 1024), BF), ((256, NLON), BF), ((512, 512), BF), ((512, 512), BF), ((512, 512), BF), ((512, 512), BF),
        ((512, 512), BF), ((512, 512), F32), ((4, 128, 512), BF), ((4, 512, 128), BF), ((4, 512, 128), BF),
        ((4, NZ, NY, NC, 16, 128), BF), ((2, 2, 8, 4, 16, 128), BF), ((2, 2, 8, 4, 16, 128), BF), ((2, 2, 8, 8, 16, 128), BF),
        ((4, NZ, NY, NC, 16, 128), BF),
        ((4, 4, 512, 128), BF), ((2, 4, 512, 128), BF),
        ((4, 384, 128), BF), ((4, 384, 128), BF), ((2, 8, 24, 128), F32), ((2, 8, 24, 128), F32),
        ((24, 128), F32), ((8, 24, 128), F32), ((24, 128), F32), ((2, 8, 24, 128), F32),
    ]
    sems = [(4, 4), (4, 6), (4, 8), (4, 5), (7,), (7,), (7,), (5,), (5,)]
    outs = [((CL, JL, NLON), BF), ((4, 128, 512), BF), ((256, NLON), BF), ((64, 256), F32), ((64, 512), F32)]
    return pl.pallas_call(
        whole_kernel,
        out_shape=tuple(jax.ShapeDtypeStruct(*o) for o in outs),
        in_specs=[SM, SM] + [VM] * (len(operands) - 2),
        out_specs=tuple(VM for _ in outs),
        scratch_shapes=[pltpu.VMEM(*s) for s in scratch] + [pltpu.SemaphoreType.DMA(s) for s in sems],
        compiler_params=pltpu.CompilerParams(vmem_limit_bytes=VMEM_BYTES, collective_id=0, has_side_effects=True),
        name="whole",
    )(*operands)


def finish_kernel(y_in, spec_in, grad_in, mix_in, gain_in, y_out, spec_out, grad_out, mix_out, gain_out):
    y_out[...] = y_in[...]
    spec_out[...] = spec_in[...]
    for j in range(JL):
        grad_out[:, j, :] = grad_in[j]
    mix_out[...] = mix_in[...]
    gain_out[...] = gain_in[...]


def finish(y, spectrum, grad, mix, gain):
    outs = [((CL, JL, NLON), BF), ((4, 128, 512), BF), ((CL, JL, NLON), BF), ((64, 256), F32), ((64, 512), F32)]
    field_part = pl.BlockSpec((16, JL, NLON), lambda i: (i, 0, 0))
    spec_part = pl.BlockSpec((1, 128, 512), lambda i: (i, 0, 0))
    mix_part = pl.BlockSpec((16, 256), lambda i: (i, 0))
    gain_part = pl.BlockSpec((16, 512), lambda i: (i, 0))
    return pl.pallas_call(
        finish_kernel,
        out_shape=tuple(jax.ShapeDtypeStruct(*o) for o in outs),
        grid=(4,),
        in_specs=[field_part, spec_part, pl.BlockSpec((JL, 16, NLON), lambda i: (0, i, 0)), mix_part, gain_part],
        out_specs=(field_part, spec_part, field_part, mix_part, gain_part),
        compiler_params=pltpu.CompilerParams(vmem_limit_bytes=VMEM_BYTES),
        name="finish",
    )(y, spectrum, grad.reshape(JL, CL, NLON), mix, gain)


def one_hot(rows):
    out = np.zeros((rows.size, rows.size), np.float32)
    out[np.arange(rows.size), rows] = 1.0
    return jnp.asarray(out, BF)


def body(grid_field, order_slots, mix_weight, degree_gain, cotangent):
    d, s, j = np.meshgrid(np.arange(32), np.arange(4), np.arange(4), indexing="ij")
    perm = one_hot((j * 128 + d * 4 + s).reshape(-1))
    s, e, j = np.meshgrid(np.arange(4), np.arange(16), np.arange(4), indexing="ij")
    turn = one_hot((e * 16 + s * 4 + j).reshape(-1))
    theta = math.pi * (np.arange(NLAT) + 0.5) / NLAT
    both = np.stack([theta, theta.reshape(8, 8, 8).transpose(1, 0, 2).reshape(-1)])
    cosv = jnp.asarray(np.cos(both).reshape(2, 4, 128), F32)
    logsin = jnp.asarray(np.log(np.sin(both)).reshape(2, 4, 128), F32)
    band = jnp.asarray(np.repeat(np.sin(theta).reshape(128, JL), CL, axis=1), F32)
    sine_col = jnp.asarray(np.repeat(np.sin(both).reshape(2, NLAT, 1), 128, axis=2), F32)
    n = np.arange(1, MODES)
    logs = jnp.asarray(np.concatenate([[0.0], np.cumsum(np.log((2.0 * n - 1.0) / (2.0 * n)))]), F32)
    out, spectrum, grad, mix, gain = whole(
        order_slots, logs, order_slots.reshape(1, MODES), cosv, logsin, band, sine_col, perm, turn,
        mix_weight, degree_gain, grid_field, cotangent,
    )
    out, spectrum, grad, mix, gain = finish(out, spectrum, grad, mix, gain)
    return out, spectrum.reshape(4, 2, CL, MODES), grad, mix.T, gain


def solution(mesh):
    placed = (P("ch", "lat", None), P(), P(), P("ch", None), P("ch", "lat", None))
    return jax.shard_map(
        body,
        mesh=mesh,
        in_specs=placed,
        out_specs=(
            P("ch", "lat", None),
            P("lat", None, "ch", None),
            P("ch", "lat", None),
            P(None, "ch"),
            P("ch", None),
        ),
        check_vma=False,
    )
```
